256 devices in a mesh: azim: 32 (over y, z), merid: 4 (over x_hi, core), wall: 2 (over x_lo).
Axes of the slice: x: 4 (x_hi: 2, x_lo: 2; x = x_hi * 2 + x_lo), y: 4, z: 8, core: 2. Of those that a mesh axis runs over, the one named last changes fastest.
Arguments:
- adjoint_in: float32 [32, 4, 2, 5, 64, 512], P('azim', 'merid', 'wall'), may hold values from -6 to 6
- source: float32 [32, 4, 2, 5, 64, 512], P('azim', 'merid', 'wall'), may hold values from -6 to 6
- jacobian: bfloat16 [32, 4, 2, 5, 5, 64, 512], P('azim', 'merid', 'wall'), may hold values from -2.6875 to 2.6875
- metric: bfloat16 [32, 4, 2, 3, 64, 512], P('azim', 'merid', 'wall'), may hold values from 0.5 to 2
- penalty: bfloat16 [32, 4, 2, 96, 512], P('azim', 'merid', 'wall'), may hold values from 0.5 to 2
- deriv: float32 [3, 64, 64], replicated, may hold values from -0.75 to 0.75
- interp: float32 [96, 64], replicated, may hold values from -0.75 to 0.75
- face_match: int32 [32, 4, 2, 4, 128], P('azim', 'merid', 'wall'), may hold values from 0 to 127, each once within a row
- orientation: int32 [32, 4, 2, 4, 128], P('azim', 'merid', 'wall'), may hold values from 0 to 7
- wall_faces: int32 [32, 4, 16], P('azim', 'merid'), may hold values from 0 to 15, as said below
- wall_geometry: bfloat16 [32, 4, 3, 5, 256], P('azim', 'merid'), may hold values from -3 to 3
- lattice_cells: int32 [32, 4, 256], P('azim', 'merid'), may hold values from 0 to 65535, as said below
- block_owner: int32 [256], replicated, may hold values from 0 to 255, each once
Outputs:
- adjoint: float32 [32, 4, 2, 5, 64, 512], P('azim', 'merid', 'wall')
- ffd_sens: float32 [3, 65536], P(None, ('azim', 'merid', 'wall'))
The draws below stay inside these ranges and needn't reach their ends.
Inputs may be any that keep to these rules, and one draw needn't show every extreme that they name: Each row of face_match along its last dimension is a permutation. `wall_faces`: the 16 entries of a row are distinct. `lattice_cells`: among the 256 points of one row (one partition), at most 2 lie in any one lattice block of 256 control points (columns b * 256 to (b + 1) * 256 - 1), and some block holds exactly 2 of them. block_owner is a permutation.
All inputs are finite; a program needn't handle non-finite values.
Results may differ from the reference program's by a relative error of at most 0.00085.
Values sent between devices are 32-bit elements; how exact they have to be, the bound alone decides.
A program may use at most 128 MiB of HBM per device.

```python
import math
import jax
import jax.numpy as jnp
from jax import lax

NV = 5
NSP = 64
FPTS = 16
NFP = 96
EX = 4
EZ = 32
EY = 4
E = 512
FACES = 128
WALLF = 16
PTS = 256
STEPS = 2
LAT = 65536
SECTORS = 32
MSLABS = 4
WSLABS = 2
BLOCK = 256
CAP = 2
DEVICES = 256


def draw_wall_faces(key, part):
    keys = jax.random.split(key, SECTORS * MSLABS)
    rows = jax.vmap(lambda one_key: jax.random.permutation(one_key, EX * EY)[:WALLF])(keys)
    return rows.reshape(SECTORS, MSLABS, WALLF).astype(jnp.int32)


def cells_row(one_key):
    first_key, second_key, third_key, fourth_key = jax.random.split(one_key, 4)
    full_block = jax.random.randint(first_key, (), 0, DEVICES, dtype=jnp.int32)
    slots = jax.random.permutation(second_key, (DEVICES - 1) * CAP)[:PTS - CAP].astype(jnp.int32)
    blocks = slots // CAP
    blocks = jnp.where(blocks >= full_block, blocks + 1, blocks)
    blocks = jnp.concatenate([jnp.full((CAP,), full_block, dtype=jnp.int32), blocks])
    blocks = jnp.take(blocks, jax.random.permutation(third_key, PTS).astype(jnp.int32))
    inside = jax.random.randint(fourth_key, (PTS,), 0, BLOCK, dtype=jnp.int32)
    return (blocks * BLOCK + inside).astype(jnp.int32)


def draw_lattice_cells(key, part):
    keys = jax.random.split(jax.random.fold_in(key, 7), SECTORS * MSLABS)
    rows = jax.vmap(cells_row)(keys)
    return rows.reshape(SECTORS, MSLABS, PTS).astype(jnp.int32)


def plant(values, rng, low, top_value):
    longest = values.shape.index(max(values.shape))
    spots = []
    for shift in (0, 1):
        where = [jax.random.randint(jax.random.fold_in(rng, axis), (), 0, length) for axis, length in enumerate(values.shape)]
        where[longest] = (where[longest] + shift) % values.shape[longest]
        spots.append(tuple(where))
    return values.at[spots[0]].set(low).at[spots[1]].set(top_value)


def shard_levels(rng, shape, shards, low, largest):
    factor_of = 1.0
    for position, blocks in shards:
        draws = jax.random.uniform(jax.random.fold_in(jax.random.fold_in(rng, 6), position), (blocks,), jnp.float32, low / len(shards), largest / len(shards))
        factor_of = factor_of * jnp.repeat(jnp.exp(draws), shape[position] // blocks).reshape((-1,) + (1,) * (len(shape) - 1 - position))
    return factor_of


def gaussian(key, extent, deviation, bound, cuts=(), held_as=jnp.bfloat16):
    values = jax.random.normal(key, extent, jnp.float32) * deviation
    if len(cuts) > 0:
        values = shard_levels(key, extent, cuts, -0.22, 0.18) * values
    return jnp.clip(values, min=-bound, max=bound).astype(held_as)


def setup_inputs(seed: int = 0) -> dict:
    key_list = jax.random.split(jax.random.key(seed), 14)
    adjoint_in = gaussian(key_list[0], (SECTORS, MSLABS, WSLABS, NV, NSP, E), 1.0, 6.0, ((0, 32), (1, 4), (2, 2)), jnp.float32)
    source = gaussian(key_list[1], (SECTORS, MSLABS, WSLABS, NV, NSP, E), 1.0, 6.0, ((0, 32), (1, 4), (2, 2)), jnp.float32)
    jacobian = gaussian(key_list[2], (SECTORS, MSLABS, WSLABS, NV, NV, NSP, E), 0.45, 2.6875, ((0, 32), (1, 4), (2, 2)))
    metric = jnp.clip(jnp.exp(math.log(2.0) - 1.3862944 * jax.random.uniform(key_list[3], (SECTORS, MSLABS, WSLABS, 3, NSP, E), jnp.float32) ** shard_levels(key_list[3], (SECTORS, MSLABS, WSLABS, 3, NSP, E), ((0, 32), (1, 4), (2, 2)), -0.2, 0.2)), 0.5, 2.0).astype(jnp.bfloat16)
    penalty = jnp.clip(jnp.exp(math.log(2.0) - 1.3862944 * jax.random.uniform(key_list[4], (SECTORS, MSLABS, WSLABS, NFP, E), jnp.float32) ** shard_levels(key_list[4], (SECTORS, MSLABS, WSLABS, NFP, E), ((0, 32), (1, 4), (2, 2)), -0.2, 0.2)), 0.5, 2.0).astype(jnp.bfloat16)
    deriv = gaussian(key_list[5], (3, NSP, NSP), NSP ** -0.5, 0.75, (), jnp.float32)
    interp = gaussian(key_list[6], (NFP, NSP), NSP ** -0.5, 0.75, (), jnp.float32)
    face_match = jax.vmap(lambda own: jax.random.permutation(own, FACES))(jax.random.split(key_list[7], SECTORS * MSLABS * WSLABS * 4)).reshape((SECTORS, MSLABS, WSLABS, 4, FACES)).astype(jnp.int32)
    orientation = plant(jax.random.randint(key_list[8], (SECTORS, MSLABS, WSLABS, 4, FACES), 0, 8), jax.random.fold_in(key_list[8], 1), 0, 7).astype(jnp.int32)
    wall_faces = draw_wall_faces(jax.random.fold_in(key_list[13], 71), 0)
    wall_geometry = gaussian(key_list[10], (SECTORS, MSLABS, 3, NV, PTS), 0.5, 3.0, ((0, 32), (1, 4)))
    lattice_cells = draw_lattice_cells(jax.random.fold_in(key_list[13], 71), 0)
    block_owner = jax.random.permutation(key_list[12], DEVICES).astype(jnp.int32)
    return {"adjoint_in": adjoint_in, "source": source, "jacobian": jacobian, "metric": metric, "penalty": penalty, "deriv": deriv, "interp": interp, "face_match": face_match, "orientation": orientation, "wall_faces": wall_faces, "wall_geometry": wall_geometry, "lattice_cells": lattice_cells, "block_owner": block_owner}


highest = lax.Precision.HIGHEST
WALL_SIGN = (1.0, 1.0, 1.0, -1.0, 1.0)


def face_counts():
    return (EY * EZ, EY * EZ, EX * EZ, EX * EZ, EX * EY, EX * EY)


def side_elements(side_no):
    faces = jnp.arange(face_counts()[side_no], dtype=jnp.int32)
    plane = EY * EZ
    if side_no == 0:
        return faces
    if side_no == 1:
        return (EX - 1) * plane + faces
    if side_no == 2:
        return (faces // EZ) * plane + faces % EZ
    if side_no == 3:
        return (faces // EZ) * plane + (EY - 1) * EZ + faces % EZ
    if side_no == 4:
        return faces * EZ
    return faces * EZ + EZ - 1


def side_slots(side_no):
    elements = jnp.arange(EX * EY * EZ, dtype=jnp.int32)
    plane = EY * EZ
    along_x = elements // plane
    along_y = (elements // EZ) % EY
    along_z = elements % EZ
    if side_no < 2:
        slot_index = elements % plane
        coord = along_x
        limit = EX
    elif side_no < 4:
        slot_index = along_x * EZ + along_z
        coord = along_y
        limit = EY
    else:
        slot_index = elements // EZ
        coord = along_z
        limit = EZ
    edge_value = 0 if side_no % 2 == 0 else limit - 1
    return coord == edge_value, slot_index


def traces_of(adjoint, interp):
    return jnp.einsum("fp,vpe->vfe", interp, adjoint, precision=highest)


def outgoing(trace_all):
    return tuple(jnp.take(trace_all[:, side_no * FPTS:(side_no + 1) * FPTS], side_elements(side_no), axis=2) for side_no in range(6))


def orient_index(code_row):
    points = jnp.arange(FPTS, dtype=jnp.int32)[:, None]
    row_i = points // 4
    col_k = points % 4
    swapped = (code_row // 4) % 2 == 1
    first = jnp.where(swapped, col_k, row_i)
    second = jnp.where(swapped, row_i, col_k)
    first = jnp.where(code_row % 2 == 1, 3 - first, first)
    second = jnp.where((code_row // 2) % 2 == 1, 3 - second, second)
    return (first * 4 + second).astype(jnp.int32)


def aligned_faces(received, match_row, code_row):
    matched = jnp.take(received, match_row, axis=2)
    return jnp.take_along_axis(matched, orient_index(code_row)[None], axis=1)


def partition_step(adjoint, trace_all, jacobian, metric, penalty, forcing, face_match, orientation, incoming, deriv, interp):
    plane = EY * EZ
    offsets = (plane, -plane, EZ, -EZ, 1, -1)
    columns = []
    for side_no in range(6):
        arrived = incoming[side_no]
        if side_no < 4:
            arrived = aligned_faces(arrived, face_match[side_no], orientation[side_no])
        partner = side_no ^ 1
        inner = jnp.roll(trace_all[:, partner * FPTS:(partner + 1) * FPTS], offsets[side_no], axis=2)
        edge_mask, slot_index = side_slots(side_no)
        columns.append(jnp.where(edge_mask, jnp.take(arrived, slot_index, axis=2), inner))
    neighbour = jnp.concatenate(columns, axis=1)
    jump = penalty.astype(jnp.float32)[None] * (trace_all - neighbour)
    slopes = jnp.einsum("dpk,vpe->dvke", deriv, adjoint, precision=highest)
    slope = jnp.sum(metric.astype(jnp.float32)[:, None] * slopes, axis=0)
    flux = jnp.sum(jacobian.astype(jnp.float32) * slope[:, None], axis=0)
    lifted = jnp.einsum("fp,vfe->vpe", interp, jump, precision=highest)
    return adjoint + 0.25 * (forcing - flux - lifted)


def wall_sensitivity(adjoint, interp, wall_list, geometry):
    chosen = jnp.take(adjoint, wall_list * EZ, axis=2)
    wall_trace = jnp.einsum("qp,vpn->vnq", interp[4 * FPTS:5 * FPTS], chosen, precision=highest)
    wall_trace = wall_trace.reshape(wall_trace.shape[0], -1)
    return jnp.sum(wall_trace[None] * geometry.astype(jnp.float32), axis=1)


def shift_open(array, upward, axis_no):
    empty = jnp.zeros_like(lax.slice_in_dim(array, 0, 1, axis=axis_no))
    size_here = array.shape[axis_no]
    if upward:
        return jnp.concatenate([empty, lax.slice_in_dim(array, 0, size_here - 1, axis=axis_no)], axis=axis_no)
    return jnp.concatenate([lax.slice_in_dim(array, 1, size_here, axis=axis_no), empty], axis=axis_no)


def reference(adjoint_in, source, jacobian, metric, penalty, deriv, interp, face_match, orientation, wall_faces, wall_geometry, lattice_cells, block_owner):
    partitions = SECTORS * MSLABS * WSLABS
    grid_shape = (SECTORS, MSLABS, WSLABS)

    def flatten(array):
        return array.reshape((partitions,) + array.shape[3:])

    sign = jnp.array(WALL_SIGN, dtype=jnp.float32)[:, None, None]
    adjoint = adjoint_in
    for sweep_no in range(STEPS):
        sends = lax.map(lambda block_now: outgoing(traces_of(block_now, interp)), flatten(adjoint))
        sends = [item.reshape(grid_shape + item.shape[1:]) for item in sends]
        incoming = (
            jnp.roll(sends[1], 1, axis=0),
            jnp.roll(sends[0], -1, axis=0),
            shift_open(sends[3], True, 1),
            shift_open(sends[2], False, 1),
            jnp.concatenate([sends[4][:, :, :1] * sign, sends[5][:, :, :-1]], axis=2),
            shift_open(sends[4], False, 2),
        )

        def one_part(items):
            block_now, jac_now, metric_now, penalty_now, forcing_now, match_now, code_now, arrived = items
            return partition_step(block_now, traces_of(block_now, interp), jac_now, metric_now, penalty_now, forcing_now, match_now, code_now, arrived, deriv, interp)

        stepped = lax.map(one_part, (flatten(adjoint), flatten(jacobian), flatten(metric), flatten(penalty), flatten(source), flatten(face_match), flatten(orientation), tuple(flatten(item) for item in incoming)))
        adjoint = stepped.reshape(adjoint_in.shape)
    bottom = adjoint[:, :, 0]
    sens = jax.vmap(jax.vmap(lambda block_now, list_now, geom_now: wall_sensitivity(block_now, interp, list_now, geom_now)))(bottom, wall_faces, wall_geometry)
    sens_all = sens.transpose(2, 0, 1, 3).reshape(3, -1)
    cell_all = lattice_cells.reshape(-1)
    lattice = jnp.zeros((3, LAT), dtype=jnp.float32).at[:, cell_all].add(sens_all)
    ordered = jnp.zeros((3, partitions, LAT // partitions), dtype=jnp.float32).at[:, block_owner, :].set(lattice.reshape(3, partitions, -1))
    return adjoint, ordered.reshape(3, LAT)
```

```python
import functools

import jax
import jax.numpy as jnp
from jax import lax
from jax.experimental import pallas as pl
from jax.experimental.pallas import tpu as pltpu
from jax.sharding import PartitionSpec as P

MESH = pl.DeviceIdType.MESH
F32, BF16, I32 = jnp.float32, jnp.bfloat16, jnp.int32

NV = 5
NSP = 64
FPTS = 16
NFP = 96
EX = 4
E = 512
PTS = 256
STEPS = 2
BLOCK = 256
TILE = 128
WALL_SIGN = (1.0, 1.0, 1.0, -1.0, 1.0)


def iota(shape, axis):
    return lax.broadcasted_iota(I32, shape, axis)


def halves(value):
    high = value.astype(BF16)
    low = (value - high.astype(F32)).astype(BF16)
    return high, low


def dot(left, right):
    return jnp.dot(left, right, preferred_element_type=F32)


def dot_nt(left, right):
    return lax.dot_general(left, right, (((1,), (1,)), ((), ())), preferred_element_type=F32)


def turn_rows():
    row = iota((8 * FPTS, 2 * FPTS), 0)
    col = iota((8 * FPTS, 2 * FPTS), 1) & (FPTS - 1)
    code, point = row >> 4, row & 15
    i, k = point >> 2, point & 3
    first = jnp.where((code & 4) != 0, k, i)
    second = jnp.where((code & 4) != 0, i, k)
    first = jnp.where((code & 1) != 0, 3 - first, first)
    second = jnp.where((code & 2) != 0, 3 - second, second)
    return (first * 4 + second == col).astype(F32).astype(BF16)


def tile_of(ref, v, side, ex):
    return ref[v, side * FPTS : (side + 1) * FPTS, ex * TILE : (ex + 1) * TILE]


def kernel(
    sizes,
    adj_hbm,
    src_hbm,
    jac_hbm,
    met_hbm,
    pen_hbm,
    deriv,
    interp_t,
    match,
    orient,
    wall_list,
    geom,
    cells,
    owner,
    out_hbm,
    ffd,
    adj,
    src,
    jac,
    met,
    pen16,
    pen,
    trace,
    slopes,
    cat,
    base,
    jump,
    jcat,
    w_trace,
    w_slope,
    w_lift,
    square,
    picker,
    sendb,
    recvb,
    zown,
    packed,
    route_mask,
    route_to,
    spread,
    offs,
    first_tx,
    first_rx,
    second_sq,
    second_tx,
    second_rx,
    load_sem,
    face_send,
    face_recv,
    one_send,
    one_recv,
    two_send,
    two_recv,
    out_sem,
):
    na, nm, nw = sizes
    group = nm * nw
    a, m, w = lax.axis_index("azim"), lax.axis_index("merid"), lax.axis_index("wall")
    here = m * nw + w

    loads = [
        pltpu.make_async_copy(hbm, vmem, load_sem.at[i])
        for i, (hbm, vmem) in enumerate(
            [(adj_hbm, adj), (pen_hbm, pen16), (met_hbm, met), (jac_hbm, jac), (src_hbm, src)]
        )
    ]
    for load in loads:
        load.start()

    for end, side in ((0, 2), (nm - 1, 3)):

        @pl.when(m == end)
        def _():
            for step in range(STEPS):
                recvb[step, side] = jnp.zeros((NV, FPTS, TILE), F32)

    barrier = pltpu.get_barrier_semaphore()

    def greet_azim(j, carry):
        pl.semaphore_signal(
            barrier, inc=1, device_id=(lax.rem(a + j, na), m, w), device_id_type=MESH
        )
        return carry

    def greet_line(j, carry):
        other = lax.rem(here + j, group)
        pl.semaphore_signal(
            barrier, inc=1, device_id=(a, other // nw, lax.rem(other, nw)), device_id_type=MESH
        )
        return carry

    lax.fori_loop(1, group, greet_line, 0)
    lax.fori_loop(1, na, greet_azim, 0)

    square[0:64, 0:96] = interp_t[...]
    high, low = halves(square[...].T[0:96, 0:64])
    w_trace[:, 0:64] = high
    w_trace[:, 64:128] = high
    w_trace[:, 128:192] = low
    for d in range(3):
        square[0:64, 0:64] = deriv[d]
        turned = square[...].T[0:64, 0:64]
        high, low = halves(turned)
        w_slope[d * 64 : (d + 1) * 64, 0:64] = high
        w_slope[d * 64 : (d + 1) * 64, 64:128] = high
        w_slope[d * 64 : (d + 1) * 64, 128:192] = low
    high, low = halves(interp_t[...])
    w_lift[0:64, 0:96] = high
    w_lift[0:64, 96:192] = high
    w_lift[64:128, 0:96] = low
    w_lift[64:128, 96:192] = low

    lane = iota((FPTS, TILE), 1)
    strip = lane >> 5
    along = lane & 31
    turner = turn_rows()

    def face_copy(step, at, side, target):
        return pltpu.make_async_remote_copy(
            src_ref=sendb.at[step, at],
            dst_ref=recvb.at[step, side],
            send_sem=face_send.at[step, at],
            recv_sem=face_recv.at[step, side],
            device_id=target,
            device_id_type=MESH,
        )

    def face_copies(step):
        return (
            face_copy(step, 0, 1, (lax.rem(a + na - 1, na), m, w)),
            face_copy(step, 1, 0, (lax.rem(a + 1, na), m, w)),
            face_copy(step, 2, 3, (a, jnp.maximum(m - 1, 0), w)),
            face_copy(step, 3, 2, (a, jnp.minimum(m + 1, nm - 1), w)),
            face_copy(step, 4, 4, (a, m, 1 - w)),
        )

    def traces(step):
        for v in range(NV):
            high, low = halves(adj[v])
            cat[v, 0:64] = high
            cat[v, 64:128] = low
            cat[v, 128:192] = high
            trace[v] = dot(w_trace[...], cat[v])

    def pack(step):
        for v in range(NV):
            sendb[step, 0, v] = tile_of(trace, v, 0, 0)
            sendb[step, 1, v] = tile_of(trace, v, 1, EX - 1)
        copies = face_copies(step)
        if step == 0:
            pl.semaphore_wait(barrier, na - 1 + group - 1)
        copies[0].start()
        copies[1].start()
        for v in range(NV):
            low_y = tile_of(trace, v, 2, 0)
            for ex in range(1, EX):
                low_y = jnp.where(strip == ex, pltpu.roll(tile_of(trace, v, 2, ex), 32 * ex, 1), low_y)
            sendb[step, 2, v] = low_y
            high_y = tile_of(trace, v, 3, EX - 1)
            for ex in range(EX - 1):
                high_y = jnp.where(
                    strip == ex, pltpu.roll(tile_of(trace, v, 3, ex), 32 * (ex + 1), 1), high_y
                )
            sendb[step, 3, v] = high_y
        pl.when(m > 0)(copies[2].start)
        pl.when(m < nm - 1)(copies[3].start)
        for v in range(NV):
            low_z = tile_of(trace, v, 4, 0)
            high_z = pltpu.roll(tile_of(trace, v, 5, 0), 97, 1)
            for ex in range(1, EX):
                low_z = jnp.where(along == ex, pltpu.roll(tile_of(trace, v, 4, ex), ex, 1), low_z)
                high_z = jnp.where(along == ex, pltpu.roll(tile_of(trace, v, 5, ex), 97 + ex, 1), high_z)
            zown[v] = low_z * WALL_SIGN[v]
            sendb[step, 4, v] = jnp.where(w == 0, high_z, low_z)
        copies[4].start()

    def inner_part(step):
        for v in range(NV):
            slopes[v] = dot(w_slope[...], cat[v])

        def chunk(i, carry):
            row = pl.multiple_of((i >> 2) * 16, 16)
            rows = pl.ds(row, 16)
            lanes = pl.ds(pl.multiple_of((i & 3) * TILE, TILE), TILE)
            metric = [met[d, rows, lanes].astype(F32) for d in range(3)]
            slope = []
            for x in range(NV):
                total = metric[0] * slopes[x, rows, lanes]
                for d in range(1, 3):
                    total = total + metric[d] * slopes[x, pl.ds(d * 64 + row, 16), lanes]
                slope.append(total)
            for u in range(NV):
                flux = jac[u, rows, lanes].astype(F32) * slope[0]
                for x in range(1, NV):
                    flux = flux + jac[x * NV + u, rows, lanes].astype(F32) * slope[x]
                base[u, rows, lanes] = adj[u, rows, lanes] + 0.25 * (src[u, rows, lanes] - flux)
            return carry

        lax.fori_loop(0, 16, chunk, 0)

        for v in range(NV):
            for ex in range(EX):
                lanes = slice(ex * TILE, (ex + 1) * TILE)
                parts = (
                    tile_of(trace, v, 1, ex - 1) if ex > 0 else None,
                    tile_of(trace, v, 0, ex + 1) if ex < EX - 1 else None,
                    jnp.where(strip == 0, 0.0, pltpu.roll(tile_of(trace, v, 3, ex), 32, 1)),
                    jnp.where(strip == 3, 0.0, pltpu.roll(tile_of(trace, v, 2, ex), 96, 1)),
                    jnp.where(along == 0, 0.0, pltpu.roll(tile_of(trace, v, 5, ex), 1, 1)),
                    jnp.where(along == 31, 0.0, pltpu.roll(tile_of(trace, v, 4, ex), 127, 1)),
                )
                for side, part in enumerate(parts):
                    rows = slice(side * FPTS, (side + 1) * FPTS)
                    own = tile_of(trace, v, side, ex)
                    jump[v, rows, lanes] = pen[rows, lanes] * (own if part is None else own - part)

    def wait_faces(step):
        copies = face_copies(step)
        copies[1].wait_recv()
        copies[0].wait_recv()
        pl.when(m > 0)(copies[3].wait_recv)
        pl.when(m < nm - 1)(copies[2].wait_recv)
        copies[4].wait_recv()

    def aligned(step, side):
        received = recvb[step, side].reshape(NV * FPTS, TILE)
        high, low = halves(received)
        matched = dot(jnp.concatenate([high, low], axis=1), picker[side])
        rows = jnp.concatenate([matched[v * FPTS : (v + 1) * FPTS] for v in range(NV)], axis=1)
        high, low = halves(rows)
        turned = dot(turner, jnp.concatenate([high, low], axis=0))
        code = orient[side : side + 1, :]
        result = []
        for v in range(NV):
            total = jnp.zeros((FPTS, TILE), F32)
            for o in range(8):
                total = jnp.where(
                    code == o, turned[o * FPTS : (o + 1) * FPTS, v * TILE : (v + 1) * TILE], total
                )
            result.append(total)
        return result

    def outer_part(step):
        arrived = [aligned(step, side) for side in range(4)]
        for v in range(NV):
            z_low = jnp.where(w == 0, zown[v], recvb[step, 4, v])
            z_high = jnp.where(w == 0, recvb[step, 4, v], 0.0)
            first = slice(0, TILE)
            last = slice(E - TILE, E)
            jump[v, 0:16, first] = jump[v, 0:16, first] - pen[0:16, first] * arrived[0][v]
            jump[v, 16:32, last] = jump[v, 16:32, last] - pen[16:32, last] * arrived[1][v]
            for ex in range(EX):
                lanes = slice(ex * TILE, (ex + 1) * TILE)
                low_y = arrived[2][v]
                high_y = arrived[3][v]
                low_y = low_y if ex == 0 else pltpu.roll(low_y, TILE - 32 * ex, 1)
                high_y = high_y if ex == EX - 1 else pltpu.roll(high_y, 96 - 32 * ex, 1)
                low_z = z_low if ex == 0 else pltpu.roll(z_low, TILE - ex, 1)
                high_z = pltpu.roll(z_high, 31 - ex, 1)
                edges = (
                    jnp.where(strip == 0, low_y, 0.0),
                    jnp.where(strip == 3, high_y, 0.0),
                    jnp.where(along == 0, low_z, 0.0),
                    jnp.where(along == 31, high_z, 0.0),
                )
                for side, edge in enumerate(edges, start=2):
                    rows = slice(side * FPTS, (side + 1) * FPTS)
                    jump[v, rows, lanes] = jump[v, rows, lanes] - pen[rows, lanes] * edge
            high, low = halves(jump[v])
            jcat[v, 0:96] = high
            jcat[v, 96:192] = low
            lifted = dot(w_lift[...], jcat[v])
            adj[v] = base[v] - 0.25 * (lifted[0:64] + lifted[64:128])

    def plan_routes():
        for side in range(4):
            pick = (iota((TILE, TILE), 0) == match[side : side + 1, :]).astype(F32).astype(BF16)
            picker[side, 0:TILE] = pick
            picker[side, TILE : 2 * TILE] = pick
        count = owner.shape[1]
        block = cells[...] >> 8
        at_block = (iota((count, PTS), 0) == block).astype(F32).astype(BF16)
        owners = jnp.broadcast_to(owner[...].astype(F32), (8, count)).astype(BF16)
        target = dot(owners, at_block)[0:1].astype(I32)
        earlier = (iota((PTS, PTS), 0) < iota((PTS, PTS), 1)).astype(F32).astype(BF16)
        before = dot(at_block, earlier)
        slot = jnp.sum(at_block.astype(F32) * before, axis=0, keepdims=True).astype(I32)
        place = target & (group - 1)
        sector = target >> (group.bit_length() - 1)
        row = iota((8 * group, PTS), 0)
        route_mask[...] = jnp.where(
            ((row >> 3) == place) & ((row & 1) == slot), 1.0, 0.0
        )
        route_to[...] = (iota((TILE, PTS), 0) == sector).astype(F32).astype(BF16)
        offs[...] = (cells[...] & (BLOCK - 1)).astype(F32)
        point = iota((1, PTS), 1) >> 4
        spot = jnp.zeros((1, PTS), I32)
        for n in range(PTS // FPTS):
            face = wall_list[n]
            spot = jnp.where(point == n, (face & 3) * 32 + (face >> 2), spot)
        pick = (iota((TILE, PTS), 0) == spot).astype(F32).astype(BF16)
        spread[0:TILE] = pick
        spread[TILE : 2 * TILE] = pick

    def wall_points():
        wide = iota((NSP, TILE), 1) & 31
        for v in range(NV):
            bottom = adj[v, :, 0:TILE]
            for ex in range(1, EX):
                bottom = jnp.where(
                    wide == ex, pltpu.roll(adj[v, :, ex * TILE : (ex + 1) * TILE], ex, 1), bottom
                )
            high, low = halves(bottom)
            lanes = slice(v * TILE, (v + 1) * TILE)
            packed[0:64, lanes] = high
            packed[64:128, lanes] = low
            packed[128:192, lanes] = high
        at_wall = dot(w_trace[4 * FPTS : 5 * FPTS], packed[...])
        rows = jnp.concatenate([at_wall[:, v * TILE : (v + 1) * TILE] for v in range(NV)], axis=0)
        high, low = halves(rows)
        expanded = dot(jnp.concatenate([high, low], axis=1), spread[...])
        own_point = (iota((FPTS, PTS), 1) & 15) == iota((FPTS, PTS), 0)
        sens = [jnp.zeros((1, PTS), F32) for c in range(3)]
        for v in range(NV):
            values = jnp.where(own_point, expanded[v * FPTS : (v + 1) * FPTS], 0.0)
            line = jnp.sum(values, axis=0, keepdims=True)
            for c in range(3):
                sens[c] = sens[c] + geom[v, c : c + 1, :].astype(F32) * line
        field = iota((8, PTS), 0) >> 1
        values = jnp.broadcast_to(offs[...], (8, PTS))
        for c in range(3):
            values = jnp.where(field == c, sens[c], values)
        high, low = halves(jnp.concatenate([values] * group, axis=0) * route_mask[...])
        routed = dot_nt(jnp.concatenate([high, low], axis=0), route_to[...])
        routed = routed[0 : 8 * group] + routed[8 * group : 16 * group]
        for g in range(group):
            first_tx[g] = routed[g * 8 : (g + 1) * 8]

    def line_copy(j):
        other = lax.rem(here + j, group)
        return pltpu.make_async_remote_copy(
            src_ref=first_tx.at[other],
            dst_ref=first_rx.at[m],
            send_sem=one_send.at[j],
            recv_sem=one_recv.at[m],
            device_id=(a, other // nw, lax.rem(other, nw)),
            device_id_type=MESH,
        )

    def line_arrival(source):
        return pltpu.make_async_remote_copy(
            src_ref=first_tx.at[0],
            dst_ref=first_rx.at[source],
            send_sem=one_send.at[0],
            recv_sem=one_recv.at[source],
            device_id=(a, m, w),
            device_id_type=MESH,
        )

    def ring_copy(j):
        other = lax.rem(a + j, na)
        return pltpu.make_async_remote_copy(
            src_ref=second_tx.at[other],
            dst_ref=second_rx.at[a],
            send_sem=two_send.at[j],
            recv_sem=two_recv.at[a],
            device_id=(other, m, w),
            device_id_type=MESH,
        )

    def ring_arrival(j):
        other = lax.rem(a + na - j, na)
        return pltpu.make_async_remote_copy(
            src_ref=second_tx.at[0],
            dst_ref=second_rx.at[other],
            send_sem=two_send.at[0],
            recv_sem=two_recv.at[other],
            device_id=(other, m, w),
            device_id_type=MESH,
        )

    loads[0].wait()
    for step in range(STEPS):
        traces(step)
        pack(step)
        if step == 0:
            plan_routes()
            for load in loads[1:]:
                load.wait()
            pen[...] = pen16[...].astype(F32)
        inner_part(step)
        wait_faces(step)
        outer_part(step)

    store = pltpu.make_async_copy(adj, out_hbm, out_sem)

    @pl.when(w == 0)
    def _():
        wall_points()
        for j in range(1, group):
            line_copy(j).start()
        first_rx[m] = first_tx[here]

    store.start()

    for source in range(nm):

        @pl.when((w != 0) | (m != source))
        def _():
            line_arrival(source).wait_recv()

    if nm * 8 < TILE:
        second_sq[nm * 8 : TILE] = jnp.zeros((TILE - nm * 8, TILE), F32)
    for source in range(nm):
        second_sq[source * 8 : (source + 1) * 8] = first_rx[source]
    second_sq[...] = second_sq[...].T
    for i in range(na):
        second_tx[i] = second_sq[i : i + 1, :]

    def send_ring(j, carry):
        ring_copy(j).start()
        return carry

    lax.fori_loop(1, na, send_ring, 0)
    second_rx[a] = second_tx[a]

    def wait_ring(j, carry):
        ring_arrival(j).wait_recv()
        return carry

    lax.fori_loop(1, na, wait_ring, 0)
    for i in range(na):
        second_sq[i : i + 1, :] = second_rx[i]
    came = second_sq[0:na, :]
    column = iota((na, BLOCK), 1).astype(F32)
    sums = [jnp.zeros((na, BLOCK), F32) for c in range(3)]
    for source in range(nm):
        for slot in range(2):
            at = source * 8 + slot
            hit = came[:, at + 6 : at + 7] == column
            for c in range(3):
                sums[c] = sums[c] + jnp.where(hit, came[:, at + 2 * c : at + 2 * c + 1], 0.0)
    for c in range(3):
        ffd[c : c + 1, :] = jnp.sum(sums[c], axis=0, keepdims=True)

    for step in range(STEPS):
        copies = face_copies(step)
        copies[0].wait_send()
        copies[1].wait_send()
        pl.when(m > 0)(copies[2].wait_send)
        pl.when(m < nm - 1)(copies[3].wait_send)
        copies[4].wait_send()

    @pl.when(w == 0)
    def _():
        for j in range(1, group):
            line_copy(j).wait_send()

    def sent_ring(j, carry):
        ring_copy(j).wait_send()
        return carry

    lax.fori_loop(1, na, sent_ring, 0)
    store.wait()


def solution(mesh):
    sizes = tuple(mesh.shape[name] for name in ("azim", "merid", "wall"))
    na, nm, nw = sizes
    group = nm * nw
    faces = (STEPS, 5, NV, FPTS, TILE)
    scratch = [
        pltpu.VMEM((NV, NSP, E), F32),
        pltpu.VMEM((NV, NSP, E), F32),
        pltpu.VMEM((NV * NV, NSP, E), BF16),
        pltpu.VMEM((3, NSP, E), BF16),
        pltpu.VMEM((NFP, E), BF16),
        pltpu.VMEM((NFP, E), F32),
        pltpu.VMEM((NV, NFP, E), F32),
        pltpu.VMEM((NV, 3 * NSP, E), F32),
        pltpu.VMEM((NV, 3 * NSP, E), BF16),
        pltpu.VMEM((NV, NSP, E), F32),
        pltpu.VMEM((NV, NFP, E), F32),
        pltpu.VMEM((NV, 2 * NFP, E), BF16),
        pltpu.VMEM((NFP, 3 * NSP), BF16),
        pltpu.VMEM((3 * NSP, 3 * NSP), BF16),
        pltpu.VMEM((2 * NSP, 2 * NFP), BF16),
        pltpu.VMEM((TILE, TILE), F32),
        pltpu.VMEM((4, 2 * TILE, TILE), BF16),
        pltpu.VMEM(faces, F32),
        pltpu.VMEM(faces, F32),
        pltpu.VMEM((NV, FPTS, TILE), F32),
        pltpu.VMEM((3 * NSP, NV * TILE), BF16),
        pltpu.VMEM((8 * group, PTS), F32),
        pltpu.VMEM((TILE, PTS), BF16),
        pltpu.VMEM((2 * TILE, PTS), BF16),
        pltpu.VMEM((1, PTS), F32),
        pltpu.VMEM((group, 8, TILE), F32),
        pltpu.VMEM((nm, 8, TILE), F32),
        pltpu.VMEM((TILE, TILE), F32),
        pltpu.VMEM((na, 1, TILE), F32),
        pltpu.VMEM((na, 1, TILE), F32),
        pltpu.SemaphoreType.DMA((5,)),
        pltpu.SemaphoreType.DMA((STEPS, 5)),
        pltpu.SemaphoreType.DMA((STEPS, 5)),
        pltpu.SemaphoreType.DMA((group,)),
        pltpu.SemaphoreType.DMA((nm,)),
        pltpu.SemaphoreType.DMA((na,)),
        pltpu.SemaphoreType.DMA((na,)),
        pltpu.SemaphoreType.DMA,
    ]
    hbm = pl.BlockSpec(memory_space=pl.ANY)
    vmem = pl.BlockSpec(memory_space=pltpu.VMEM)
    smem = pl.BlockSpec(memory_space=pltpu.SMEM)
    call = pl.pallas_call(
        functools.partial(kernel, sizes),
        out_shape=(
            jax.ShapeDtypeStruct((NV, NSP, E), F32),
            jax.ShapeDtypeStruct((3, BLOCK), F32),
        ),
        in_specs=[hbm] * 5 + [vmem] * 4 + [smem] + [vmem] * 3,
        out_specs=(hbm, vmem),
        scratch_shapes=scratch,
        compiler_params=pltpu.CompilerParams(
            collective_id=0, has_side_effects=True, vmem_limit_bytes=40 * 1024 * 1024
        ),
        name="adjoint_steps",
    )

    def per_device(
        adjoint_in,
        source,
        jacobian,
        metric,
        penalty,
        deriv,
        interp,
        face_match,
        orientation,
        wall_faces,
        wall_geometry,
        lattice_cells,
        block_owner,
    ):
        adjoint, owned = call(
            adjoint_in.reshape(NV, NSP, E),
            source.reshape(NV, NSP, E),
            jacobian.reshape(NV * NV, NSP, E),
            metric.reshape(3, NSP, E),
            penalty.reshape(NFP, E),
            deriv,
            interp.T,
            face_match.reshape(4, TILE),
            orientation.reshape(4, TILE),
            wall_faces.reshape(-1),
            wall_geometry.reshape(3, NV, PTS).transpose(1, 0, 2),
            lattice_cells.reshape(1, PTS),
            block_owner.reshape(1, -1),
        )
        return adjoint[None, None, None], owned

    placed = (
        P("azim", "merid", "wall", None, None, None),
        P("azim", "merid", "wall", None, None, None),
        P("azim", "merid", "wall", None, None, None, None),
        P("azim", "merid", "wall", None, None, None),
        P("azim", "merid", "wall", None, None),
        P(),
        P(),
        P("azim", "merid", "wall", None, None),
        P("azim", "merid", "wall", None, None),
        P("azim", "merid", None),
        P("azim", "merid", None, None, None),
        P("azim", "merid", None),
        P(),
    )
    return jax.shard_map(
        per_device,
        mesh=mesh,
        in_specs=placed,
        out_specs=(
            P("azim", "merid", "wall", None, None, None),
            P(None, ("azim", "merid", "wall")),
        ),
        check_vma=False,
    )
```

```python
import functools

import jax
import jax.numpy as jnp
from jax import lax
from jax.experimental import pallas as pl
from jax.experimental.pallas import tpu as pltpu
from jax.sharding import PartitionSpec as P

MESH = pl.DeviceIdType.MESH
F32, BF16, I32 = jnp.float32, jnp.bfloat16, jnp.int32

NV = 5
NSP = 64
FPTS = 16
NFP = 96
EX = 4
E = 512
PTS = 256
STEPS = 2
BLOCK = 256
TILE = 128
WALL_SIGN = (1.0, 1.0, 1.0, -1.0, 1.0)


def iota(shape, axis):
    return lax.broadcasted_iota(I32, shape, axis)


def halves(value):
    high = value.astype(BF16)
    low = (value - high.astype(F32)).astype(BF16)
    return high, low


def dot(left, right):
    return jnp.dot(left, right, preferred_element_type=F32)


def dot_nt(left, right):
    return lax.dot_general(left, right, (((1,), (1,)), ((), ())), preferred_element_type=F32)


def turn_rows():
    row = iota((8 * FPTS, 2 * FPTS), 0)
    col = iota((8 * FPTS, 2 * FPTS), 1) & (FPTS - 1)
    code, point = row >> 4, row & 15
    i, k = point >> 2, point & 3
    first = jnp.where((code & 4) != 0, k, i)
    second = jnp.where((code & 4) != 0, i, k)
    first = jnp.where((code & 1) != 0, 3 - first, first)
    second = jnp.where((code & 2) != 0, 3 - second, second)
    return (first * 4 + second == col).astype(F32).astype(BF16)


def tile_of(ref, v, side, ex):
    return ref[v, side * FPTS : (side + 1) * FPTS, ex * TILE : (ex + 1) * TILE]


def kernel(
    sizes,
    adj_hbm,
    src_hbm,
    jac_hbm,
    met_hbm,
    pen_hbm,
    deriv_hbm,
    interp_hbm,
    match_hbm,
    orient_hbm,
    list_hbm,
    geom_hbm,
    cells_hbm,
    owner_hbm,
    out_hbm,
    ffd,
    adj,
    src,
    jac,
    met,
    pen16,
    deriv,
    interp_t,
    match,
    orient,
    wall_list,
    geom,
    cells,
    owner,
    pen,
    trace,
    slopes,
    cat,
    base,
    jump,
    jcat,
    w_trace,
    w_slope,
    w_lift,
    square,
    picker,
    sendb,
    recvb,
    zown,
    packed,
    route_mask,
    route_to,
    spread,
    offs,
    first_tx,
    first_rx,
    second_sq,
    second_tx,
    second_rx,
    load_sem,
    face_send,
    face_recv,
    one_send,
    one_recv,
    two_send,
    two_recv,
    out_sem,
):
    na, nm, nw = sizes
    group = nm * nw
    a, m, w = lax.axis_index("azim"), lax.axis_index("merid"), lax.axis_index("wall")
    here = m * nw + w

    pairs = (
        (interp_hbm, interp_t),
        (adj_hbm, adj),
        (deriv_hbm, deriv),
        (match_hbm, match),
        (cells_hbm, cells),
        (owner_hbm, owner),
        (list_hbm, wall_list),
        (pen_hbm, pen16),
        (met_hbm, met),
        (jac_hbm, jac),
        (src_hbm, src),
        (orient_hbm, orient),
        (geom_hbm, geom),
    )
    loads = [pltpu.make_async_copy(*pair, load_sem.at[i]) for i, pair in enumerate(pairs)]
    for load in loads:
        load.start()

    for end, side in ((0, 2), (nm - 1, 3)):

        @pl.when(m == end)
        def _():
            for step in range(STEPS):
                recvb[step, side] = jnp.zeros((NV, FPTS, TILE), F32)

    barrier = pltpu.get_barrier_semaphore()

    def greet_azim(j, carry):
        pl.semaphore_signal(
            barrier, inc=1, device_id=(lax.rem(a + j, na), m, w), device_id_type=MESH
        )
        return carry

    def greet_line(j, carry):
        other = lax.rem(here + j, group)
        pl.semaphore_signal(
            barrier, inc=1, device_id=(a, other // nw, lax.rem(other, nw)), device_id_type=MESH
        )
        return carry

    lax.fori_loop(1, group, greet_line, 0)
    lax.fori_loop(1, na, greet_azim, 0)

    lane = iota((FPTS, TILE), 1)
    strip = lane >> 5
    along = lane & 31
    turner = turn_rows()

    def interp_operators():
        square[0:64, 0:96] = interp_t[...]
        high, low = halves(square[...].T[0:96, 0:64])
        w_trace[:, 0:64] = high
        w_trace[:, 64:128] = high
        w_trace[:, 128:192] = low
        high, low = halves(interp_t[...])
        w_lift[0:64, 0:96] = high
        w_lift[0:64, 96:192] = high
        w_lift[64:128, 0:96] = low
        w_lift[64:128, 96:192] = low

    def deriv_operators():
        for d in range(3):
            square[0:64, 0:64] = deriv[d]
            high, low = halves(square[...].T[0:64, 0:64])
            w_slope[d * 64 : (d + 1) * 64, 0:64] = high
            w_slope[d * 64 : (d + 1) * 64, 64:128] = high
            w_slope[d * 64 : (d + 1) * 64, 128:192] = low

    def face_copy(step, at, side, target):
        return pltpu.make_async_remote_copy(
            src_ref=sendb.at[step, at],
            dst_ref=recvb.at[step, side],
            send_sem=face_send.at[step, at],
            recv_sem=face_recv.at[step, side],
            device_id=target,
            device_id_type=MESH,
        )

    def face_copies(step):
        return (
            face_copy(step, 0, 1, (lax.rem(a + na - 1, na), m, w)),
            face_copy(step, 1, 0, (lax.rem(a + 1, na), m, w)),
            face_copy(step, 2, 3, (a, jnp.maximum(m - 1, 0), w)),
            face_copy(step, 3, 2, (a, jnp.minimum(m + 1, nm - 1), w)),
            face_copy(step, 4, 4, (a, m, 1 - w)),
        )

    def traces(step):
        for v in range(NV):
            high, low = halves(adj[v])
            cat[v, 0:64] = high
            cat[v, 64:128] = low
            cat[v, 128:192] = high
            trace[v] = dot(w_trace[...], cat[v])

    def pack(step):
        for v in range(NV):
            sendb[step, 0, v] = tile_of(trace, v, 0, 0)
            sendb[step, 1, v] = tile_of(trace, v, 1, EX - 1)
        copies = face_copies(step)
        if step == 0:
            pl.semaphore_wait(barrier, na - 1 + group - 1)
        copies[0].start()
        copies[1].start()
        for v in range(NV):
            low_y = tile_of(trace, v, 2, 0)
            for ex in range(1, EX):
                low_y = jnp.where(strip == ex, pltpu.roll(tile_of(trace, v, 2, ex), 32 * ex, 1), low_y)
            sendb[step, 2, v] = low_y
            high_y = tile_of(trace, v, 3, EX - 1)
            for ex in range(EX - 1):
                high_y = jnp.where(
                    strip == ex, pltpu.roll(tile_of(trace, v, 3, ex), 32 * (ex + 1), 1), high_y
                )
            sendb[step, 3, v] = high_y
        pl.when(m > 0)(copies[2].start)
        pl.when(m < nm - 1)(copies[3].start)
        for v in range(NV):
            low_z = tile_of(trace, v, 4, 0)
            high_z = pltpu.roll(tile_of(trace, v, 5, 0), 97, 1)
            for ex in range(1, EX):
                low_z = jnp.where(along == ex, pltpu.roll(tile_of(trace, v, 4, ex), ex, 1), low_z)
                high_z = jnp.where(along == ex, pltpu.roll(tile_of(trace, v, 5, ex), 97 + ex, 1), high_z)
            zown[v] = low_z * WALL_SIGN[v]
            sendb[step, 4, v] = jnp.where(w == 0, high_z, low_z)
        copies[4].start()

    def inner_part(step):
        for v in range(NV):
            slopes[v] = dot(w_slope[...], cat[v])

        def chunk(i, carry):
            row = pl.multiple_of((i >> 2) * 16, 16)
            rows = pl.ds(row, 16)
            lanes = pl.ds(pl.multiple_of((i & 3) * TILE, TILE), TILE)
            metric = [met[d, rows, lanes].astype(F32) for d in range(3)]
            slope = []
            for x in range(NV):
                total = metric[0] * slopes[x, rows, lanes]
                for d in range(1, 3):
                    total = total + metric[d] * slopes[x, pl.ds(d * 64 + row, 16), lanes]
                slope.append(total)
            for u in range(NV):
                flux = jac[u, rows, lanes].astype(F32) * slope[0]
                for x in range(1, NV):
                    flux = flux + jac[x * NV + u, rows, lanes].astype(F32) * slope[x]
                base[u, rows, lanes] = adj[u, rows, lanes] + 0.25 * (src[u, rows, lanes] - flux)
            return carry

        lax.fori_loop(0, 16, chunk, 0)

        for v in range(NV):
            for ex in range(EX):
                lanes = slice(ex * TILE, (ex + 1) * TILE)
                parts = (
                    tile_of(trace, v, 1, ex - 1) if ex > 0 else None,
                    tile_of(trace, v, 0, ex + 1) if ex < EX - 1 else None,
                    jnp.where(strip == 0, 0.0, pltpu.roll(tile_of(trace, v, 3, ex), 32, 1)),
                    jnp.where(strip == 3, 0.0, pltpu.roll(tile_of(trace, v, 2, ex), 96, 1)),
                    jnp.where(along == 0, 0.0, pltpu.roll(tile_of(trace, v, 5, ex), 1, 1)),
                    jnp.where(along == 31, 0.0, pltpu.roll(tile_of(trace, v, 4, ex), 127, 1)),
                )
                for side, part in enumerate(parts):
                    rows = slice(side * FPTS, (side + 1) * FPTS)
                    own = tile_of(trace, v, side, ex)
                    jump[v, rows, lanes] = pen[rows, lanes] * (own if part is None else own - part)

    def wait_faces(step):
        copies = face_copies(step)
        copies[1].wait_recv()
        copies[0].wait_recv()
        pl.when(m > 0)(copies[3].wait_recv)
        pl.when(m < nm - 1)(copies[2].wait_recv)
        copies[4].wait_recv()

    def aligned(step, side):
        received = recvb[step, side].reshape(NV * FPTS, TILE)
        high, low = halves(received)
        matched = dot(jnp.concatenate([high, low], axis=1), picker[side])
        rows = jnp.concatenate([matched[v * FPTS : (v + 1) * FPTS] for v in range(NV)], axis=1)
        high, low = halves(rows)
        turned = dot(turner, jnp.concatenate([high, low], axis=0))
        code = orient[side : side + 1, :]
        result = []
        for v in range(NV):
            total = jnp.zeros((FPTS, TILE), F32)
            for o in range(8):
                total = jnp.where(
                    code == o, turned[o * FPTS : (o + 1) * FPTS, v * TILE : (v + 1) * TILE], total
                )
            result.append(total)
        return result

    def outer_part(step):
        arrived = [aligned(step, side) for side in range(4)]
        for v in range(NV):
            z_low = jnp.where(w == 0, zown[v], recvb[step, 4, v])
            z_high = jnp.where(w == 0, recvb[step, 4, v], 0.0)
            first = slice(0, TILE)
            last = slice(E - TILE, E)
            jump[v, 0:16, first] = jump[v, 0:16, first] - pen[0:16, first] * arrived[0][v]
            jump[v, 16:32, last] = jump[v, 16:32, last] - pen[16:32, last] * arrived[1][v]
            for ex in range(EX):
                lanes = slice(ex * TILE, (ex + 1) * TILE)
                low_y = arrived[2][v]
                high_y = arrived[3][v]
                low_y = low_y if ex == 0 else pltpu.roll(low_y, TILE - 32 * ex, 1)
                high_y = high_y if ex == EX - 1 else pltpu.roll(high_y, 96 - 32 * ex, 1)
                low_z = z_low if ex == 0 else pltpu.roll(z_low, TILE - ex, 1)
                high_z = pltpu.roll(z_high, 31 - ex, 1)
                edges = (
                    jnp.where(strip == 0, low_y, 0.0),
                    jnp.where(strip == 3, high_y, 0.0),
                    jnp.where(along == 0, low_z, 0.0),
                    jnp.where(along == 31, high_z, 0.0),
                )
                for side, edge in enumerate(edges, start=2):
                    rows = slice(side * FPTS, (side + 1) * FPTS)
                    jump[v, rows, lanes] = jump[v, rows, lanes] - pen[rows, lanes] * edge
            high, low = halves(jump[v])
            jcat[v, 0:96] = high
            jcat[v, 96:192] = low
            lifted = dot(w_lift[...], jcat[v])
            adj[v] = base[v] - 0.25 * (lifted[0:64] + lifted[64:128])

    def plan_routes():
        for side in range(4):
            pick = (iota((TILE, TILE), 0) == match[side : side + 1, :]).astype(F32).astype(BF16)
            picker[side, 0:TILE] = pick
            picker[side, TILE : 2 * TILE] = pick
        count = owner.shape[1]
        block = cells[...] >> 8
        at_block = (iota((count, PTS), 0) == block).astype(F32).astype(BF16)
        owners = jnp.broadcast_to(owner[...].astype(F32), (8, count)).astype(BF16)
        target = dot(owners, at_block)[0:1].astype(I32)
        earlier = (iota((PTS, PTS), 0) < iota((PTS, PTS), 1)).astype(F32).astype(BF16)
        before = dot(at_block, earlier)
        slot = jnp.sum(at_block.astype(F32) * before, axis=0, keepdims=True).astype(I32)
        place = target & (group - 1)
        sector = target >> (group.bit_length() - 1)
        row = iota((8 * group, PTS), 0)
        route_mask[...] = jnp.where(
            ((row >> 3) == place) & ((row & 1) == slot), 1.0, 0.0
        )
        route_to[...] = (iota((TILE, PTS), 0) == sector).astype(F32).astype(BF16)
        offs[...] = (cells[...] & (BLOCK - 1)).astype(F32)
        point = iota((1, PTS), 1) >> 4
        spot = jnp.zeros((1, PTS), I32)
        for n in range(PTS // FPTS):
            face = wall_list[n]
            spot = jnp.where(point == n, (face & 3) * 32 + (face >> 2), spot)
        pick = (iota((TILE, PTS), 0) == spot).astype(F32).astype(BF16)
        spread[0:TILE] = pick
        spread[TILE : 2 * TILE] = pick

    def wall_points():
        wide = iota((NSP, TILE), 1) & 31
        for v in range(NV):
            bottom = adj[v, :, 0:TILE]
            for ex in range(1, EX):
                bottom = jnp.where(
                    wide == ex, pltpu.roll(adj[v, :, ex * TILE : (ex + 1) * TILE], ex, 1), bottom
                )
            high, low = halves(bottom)
            lanes = slice(v * TILE, (v + 1) * TILE)
            packed[0:64, lanes] = high
            packed[64:128, lanes] = low
            packed[128:192, lanes] = high
        at_wall = dot(w_trace[4 * FPTS : 5 * FPTS], packed[...])
        rows = jnp.concatenate([at_wall[:, v * TILE : (v + 1) * TILE] for v in range(NV)], axis=0)
        high, low = halves(rows)
        expanded = dot(jnp.concatenate([high, low], axis=1), spread[...])
        own_point = (iota((FPTS, PTS), 1) & 15) == iota((FPTS, PTS), 0)
        sens = [jnp.zeros((1, PTS), F32) for c in range(3)]
        for v in range(NV):
            values = jnp.where(own_point, expanded[v * FPTS : (v + 1) * FPTS], 0.0)
            line = jnp.sum(values, axis=0, keepdims=True)
            for c in range(3):
                sens[c] = sens[c] + geom[v, c : c + 1, :].astype(F32) * line
        field = iota((8, PTS), 0) >> 1
        values = jnp.broadcast_to(offs[...], (8, PTS))
        for c in range(3):
            values = jnp.where(field == c, sens[c], values)
        high, low = halves(jnp.concatenate([values] * group, axis=0) * route_mask[...])
        routed = dot_nt(jnp.concatenate([high, low], axis=0), route_to[...])
        routed = routed[0 : 8 * group] + routed[8 * group : 16 * group]
        for g in range(group):
            first_tx[g] = routed[g * 8 : (g + 1) * 8]

    def line_copy(j):
        other = lax.rem(here + j, group)
        return pltpu.make_async_remote_copy(
            src_ref=first_tx.at[other],
            dst_ref=first_rx.at[m],
            send_sem=one_send.at[j],
            recv_sem=one_recv.at[m],
            device_id=(a, other // nw, lax.rem(other, nw)),
            device_id_type=MESH,
        )

    def line_arrival(source):
        return pltpu.make_async_remote_copy(
            src_ref=first_tx.at[0],
            dst_ref=first_rx.at[source],
            send_sem=one_send.at[0],
            recv_sem=one_recv.at[source],
            device_id=(a, m, w),
            device_id_type=MESH,
        )

    def ring_copy(j):
        other = lax.rem(a + j, na)
        return pltpu.make_async_remote_copy(
            src_ref=second_tx.at[other],
            dst_ref=second_rx.at[a],
            send_sem=two_send.at[j],
            recv_sem=two_recv.at[a],
            device_id=(other, m, w),
            device_id_type=MESH,
        )

    def ring_arrival(j):
        other = lax.rem(a + na - j, na)
        return pltpu.make_async_remote_copy(
            src_ref=second_tx.at[0],
            dst_ref=second_rx.at[other],
            send_sem=two_send.at[0],
            recv_sem=two_recv.at[other],
            device_id=(other, m, w),
            device_id_type=MESH,
        )

    loads[0].wait()
    interp_operators()
    loads[1].wait()
    for step in range(STEPS):
        traces(step)
        pack(step)
        if step == 0:
            for load in loads[2:7]:
                load.wait()
            deriv_operators()
            plan_routes()
            for load in loads[7:]:
                load.wait()
            pen[...] = pen16[...].astype(F32)
        inner_part(step)
        wait_faces(step)
        outer_part(step)

    store = pltpu.make_async_copy(adj, out_hbm, out_sem)

    @pl.when(w == 0)
    def _():
        wall_points()
        for j in range(1, group):
            line_copy(j).start()
        first_rx[m] = first_tx[here]

    store.start()

    for source in range(nm):

        @pl.when((w != 0) | (m != source))
        def _():
            line_arrival(source).wait_recv()

    if nm * 8 < TILE:
        second_sq[nm * 8 : TILE] = jnp.zeros((TILE - nm * 8, TILE), F32)
    for source in range(nm):
        second_sq[source * 8 : (source + 1) * 8] = first_rx[source]
    second_sq[...] = second_sq[...].T
    for i in range(na):
        second_tx[i] = second_sq[i : i + 1, :]

    def send_ring(j, carry):
        ring_copy(j).start()
        return carry

    lax.fori_loop(1, na, send_ring, 0)
    second_rx[a] = second_tx[a]

    def wait_ring(j, carry):
        ring_arrival(j).wait_recv()
        return carry

    lax.fori_loop(1, na, wait_ring, 0)
    for i in range(na):
        second_sq[i : i + 1, :] = second_rx[i]
    came = second_sq[0:na, :]
    column = iota((na, BLOCK), 1).astype(F32)
    sums = [jnp.zeros((na, BLOCK), F32) for c in range(3)]
    for source in range(nm):
        for slot in range(2):
            at = source * 8 + slot
            hit = came[:, at + 6 : at + 7] == column
            for c in range(3):
                sums[c] = sums[c] + jnp.where(hit, came[:, at + 2 * c : at + 2 * c + 1], 0.0)
    for c in range(3):
        ffd[c : c + 1, :] = jnp.sum(sums[c], axis=0, keepdims=True)

    for step in range(STEPS):
        copies = face_copies(step)
        copies[0].wait_send()
        copies[1].wait_send()
        pl.when(m > 0)(copies[2].wait_send)
        pl.when(m < nm - 1)(copies[3].wait_send)
        copies[4].wait_send()

    @pl.when(w == 0)
    def _():
        for j in range(1, group):
            line_copy(j).wait_send()

    def sent_ring(j, carry):
        ring_copy(j).wait_send()
        return carry

    lax.fori_loop(1, na, sent_ring, 0)
    store.wait()


def solution(mesh):
    sizes = tuple(mesh.shape[name] for name in ("azim", "merid", "wall"))
    na, nm, nw = sizes
    group = nm * nw
    faces = (STEPS, 5, NV, FPTS, TILE)
    scratch = [
        pltpu.VMEM((NV, NSP, E), F32),
        pltpu.VMEM((NV, NSP, E), F32),
        pltpu.VMEM((NV * NV, NSP, E), BF16),
        pltpu.VMEM((3, NSP, E), BF16),
        pltpu.VMEM((NFP, E), BF16),
        pltpu.VMEM((3, NSP, NSP), F32),
        pltpu.VMEM((NSP, NFP), F32),
        pltpu.VMEM((4, TILE), I32),
        pltpu.VMEM((4, TILE), I32),
        pltpu.SMEM((PTS // FPTS,), I32),
        pltpu.VMEM((NV, 3, PTS), BF16),
        pltpu.VMEM((1, PTS), I32),
        pltpu.VMEM((1, na * group), I32),
        pltpu.VMEM((NFP, E), F32),
        pltpu.VMEM((NV, NFP, E), F32),
        pltpu.VMEM((NV, 3 * NSP, E), F32),
        pltpu.VMEM((NV, 3 * NSP, E), BF16),
        pltpu.VMEM((NV, NSP, E), F32),
        pltpu.VMEM((NV, NFP, E), F32),
        pltpu.VMEM((NV, 2 * NFP, E), BF16),
        pltpu.VMEM((NFP, 3 * NSP), BF16),
        pltpu.VMEM((3 * NSP, 3 * NSP), BF16),
        pltpu.VMEM((2 * NSP, 2 * NFP), BF16),
        pltpu.VMEM((TILE, TILE), F32),
        pltpu.VMEM((4, 2 * TILE, TILE), BF16),
        pltpu.VMEM(faces, F32),
        pltpu.VMEM(faces, F32),
        pltpu.VMEM((NV, FPTS, TILE), F32),
        pltpu.VMEM((3 * NSP, NV * TILE), BF16),
        pltpu.VMEM((8 * group, PTS), F32),
        pltpu.VMEM((TILE, PTS), BF16),
        pltpu.VMEM((2 * TILE, PTS), BF16),
        pltpu.VMEM((1, PTS), F32),
        pltpu.VMEM((group, 8, TILE), F32),
        pltpu.VMEM((nm, 8, TILE), F32),
        pltpu.VMEM((TILE, TILE), F32),
        pltpu.VMEM((na, 1, TILE), F32),
        pltpu.VMEM((na, 1, TILE), F32),
        pltpu.SemaphoreType.DMA((13,)),
        pltpu.SemaphoreType.DMA((STEPS, 5)),
        pltpu.SemaphoreType.DMA((STEPS, 5)),
        pltpu.SemaphoreType.DMA((group,)),
        pltpu.SemaphoreType.DMA((nm,)),
        pltpu.SemaphoreType.DMA((na,)),
        pltpu.SemaphoreType.DMA((na,)),
        pltpu.SemaphoreType.DMA,
    ]
    hbm = pl.BlockSpec(memory_space=pltpu.HBM)
    vmem = pl.BlockSpec(memory_space=pltpu.VMEM)
    call = pl.pallas_call(
        functools.partial(kernel, sizes),
        out_shape=(
            jax.ShapeDtypeStruct((NV, NSP, E), F32),
            jax.ShapeDtypeStruct((3, BLOCK), F32),
        ),
        in_specs=[hbm] * 13,
        out_specs=(hbm, vmem),
        scratch_shapes=scratch,
        compiler_params=pltpu.CompilerParams(
            collective_id=0, has_side_effects=True, vmem_limit_bytes=60 * 1024 * 1024
        ),
        name="adjoint_steps",
    )

    def per_device(
        adjoint_in,
        source,
        jacobian,
        metric,
        penalty,
        deriv,
        interp,
        face_match,
        orientation,
        wall_faces,
        wall_geometry,
        lattice_cells,
        block_owner,
    ):
        adjoint, owned = call(
            adjoint_in.reshape(NV, NSP, E),
            source.reshape(NV, NSP, E),
            jacobian.reshape(NV * NV, NSP, E),
            metric.reshape(3, NSP, E),
            penalty.reshape(NFP, E),
            deriv,
            interp.T,
            face_match.reshape(4, TILE),
            orientation.reshape(4, TILE),
            wall_faces.reshape(-1),
            wall_geometry.reshape(3, NV, PTS).transpose(1, 0, 2),
            lattice_cells.reshape(1, PTS),
            block_owner.reshape(1, -1),
        )
        return adjoint[None, None, None], owned

    placed = (
        P("azim", "merid", "wall", None, None, None),
        P("azim", "merid", "wall", None, None, None),
        P("azim", "merid", "wall", None, None, None, None),
        P("azim", "merid", "wall", None, None, None),
        P("azim", "merid", "wall", None, None),
        P(),
        P(),
        P("azim", "merid", "wall", None, None),
        P("azim", "merid", "wall", None, None),
        P("azim", "merid", None),
        P("azim", "merid", None, None, None),
        P("azim", "merid", None),
        P(),
    )
    return jax.shard_map(
        per_device,
        mesh=mesh,
        in_specs=placed,
        out_specs=(
            P("azim", "merid", "wall", None, None, None),
            P(None, ("azim", "merid", "wall")),
        ),
        check_vma=False,
    )
```

```python
import functools

import jax
import jax.numpy as jnp
from jax import lax
from jax.experimental import pallas as pl
from jax.experimental.pallas import tpu as pltpu
from jax.sharding import PartitionSpec as P

MESH = pl.DeviceIdType.MESH
F32, BF16, I32 = jnp.float32, jnp.bfloat16, jnp.int32

NV = 5
NSP = 64
FPTS = 16
NFP = 96
EX = 4
E = 512
PTS = 256
STEPS = 2
BLOCK = 256
TILE = 128
WALL_SIGN = (1.0, 1.0, 1.0, -1.0, 1.0)


def iota(shape, axis):
    return lax.broadcasted_iota(I32, shape, axis)


def halves(value):
    high = value.astype(BF16)
    low = (value - high.astype(F32)).astype(BF16)
    return high, low


def dot(left, right):
    return jnp.dot(left, right, preferred_element_type=F32)


def dot_nt(left, right):
    return lax.dot_general(left, right, (((1,), (1,)), ((), ())), preferred_element_type=F32)


def turn_rows():
    row = iota((8 * FPTS, 2 * FPTS), 0)
    col = iota((8 * FPTS, 2 * FPTS), 1) & (FPTS - 1)
    code, point = row >> 4, row & 15
    i, k = point >> 2, point & 3
    first = jnp.where((code & 4) != 0, k, i)
    second = jnp.where((code & 4) != 0, i, k)
    first = jnp.where((code & 1) != 0, 3 - first, first)
    second = jnp.where((code & 2) != 0, 3 - second, second)
    return (first * 4 + second == col).astype(F32).astype(BF16)


def tile_of(ref, v, side, ex):
    return ref[v, side * FPTS : (side + 1) * FPTS, ex * TILE : (ex + 1) * TILE]


def kernel(
    sizes,
    adj_hbm,
    src_hbm,
    jac_hbm,
    met_hbm,
    pen_hbm,
    deriv_hbm,
    interp_hbm,
    match_hbm,
    orient_hbm,
    list_hbm,
    geom_hbm,
    cells_hbm,
    owner_hbm,
    out,
    ffd,
    adj,
    src,
    jac,
    met,
    pen16,
    deriv,
    interp_t,
    match,
    orient,
    wall_list,
    geom,
    cells,
    owner,
    pen,
    trace,
    slopes,
    cat,
    base,
    jump,
    jcat,
    w_trace,
    w_slope,
    w_lift,
    square,
    picker,
    sendb,
    recvb,
    zown,
    packed,
    route_mask,
    route_to,
    spread,
    offs,
    first_tx,
    first_rx,
    second_sq,
    second_tx,
    second_rx,
    load_sem,
    face_send,
    face_recv,
    hop_sem,
):
    na, nm, nw = sizes
    group = nm * nw
    a, m, w = lax.axis_index("azim"), lax.axis_index("merid"), lax.axis_index("wall")
    here = m * nw + w

    groups = (
        ((interp_hbm, interp_t),),
        ((adj_hbm, adj),),
        (
            (deriv_hbm, deriv),
            (match_hbm, match),
            (cells_hbm, cells),
            (owner_hbm, owner),
            (list_hbm, wall_list),
        ),
        (
            (pen_hbm, pen16),
            (met_hbm, met),
            (jac_hbm, jac),
            (src_hbm, src),
            (orient_hbm, orient),
            (geom_hbm, geom),
        ),
    )
    loads = [
        [pltpu.make_async_copy(*pair, load_sem.at[i]) for pair in group_here]
        for i, group_here in enumerate(groups)
    ]
    for part in loads:
        for load in part:
            load.start()

    def loaded(part):
        for load in loads[part]:
            load.wait()

    for end, side in ((0, 3), (nm - 1, 4)):

        @pl.when(m == end)
        def _():
            for step in range(STEPS):
                recvb[step, side] = jnp.zeros((NV, FPTS, TILE), F32)

    barrier = pltpu.get_barrier_semaphore()

    def greet_azim(j, carry):
        pl.semaphore_signal(
            barrier, inc=1, device_id=(lax.rem(a + j, na), m, w), device_id_type=MESH
        )
        return carry

    def greet_line(j, carry):
        other = lax.rem(here + j, group)
        pl.semaphore_signal(
            barrier, inc=1, device_id=(a, other // nw, lax.rem(other, nw)), device_id_type=MESH
        )
        return carry

    lax.fori_loop(1, group, greet_line, 0)
    lax.fori_loop(1, na, greet_azim, 0)

    lane = iota((FPTS, TILE), 1)
    strip = lane >> 5
    along = lane & 31
    turner = turn_rows()

    def interp_operators():
        square[0:64, 0:96] = interp_t[...]
        high, low = halves(square[...].T[0:96, 0:64])
        w_trace[:, 0:64] = high
        w_trace[:, 64:128] = high
        w_trace[:, 128:192] = low
        high, low = halves(interp_t[...])
        w_lift[0:64, 0:96] = high
        w_lift[0:64, 96:192] = high
        w_lift[64:128, 0:96] = low
        w_lift[64:128, 96:192] = low

    def deriv_operators():
        for d in range(3):
            square[0:64, 0:64] = deriv[d]
            high, low = halves(square[...].T[0:64, 0:64])
            w_slope[d * 64 : (d + 1) * 64, 0:64] = high
            w_slope[d * 64 : (d + 1) * 64, 64:128] = high
            w_slope[d * 64 : (d + 1) * 64, 128:192] = low

    def face_copy(step, at, side, target):
        return pltpu.make_async_remote_copy(
            src_ref=sendb.at[step, at],
            dst_ref=recvb.at[step, side],
            send_sem=face_send.at[max(at - 2, 0)],
            recv_sem=face_recv.at[step, max(side - 2, 0)],
            device_id=target,
            device_id_type=MESH,
        )

    def face_copies(step):
        return (
            face_copy(step, 0, 1, (lax.rem(a + na - 1, na), m, w)),
            face_copy(step, 1, 0, (lax.rem(a + 1, na), m, w)),
            face_copy(step, 2, 2, (a, m, 1 - w)),
            face_copy(step, 3, 4, (a, jnp.maximum(m - 1, 0), w)),
            face_copy(step, 4, 3, (a, jnp.minimum(m + 1, nm - 1), w)),
        )

    def three_faces(step):
        return pltpu.make_async_remote_copy(
            src_ref=sendb.at[step, 0:3],
            dst_ref=recvb.at[step, 0:3],
            send_sem=face_send.at[0],
            recv_sem=face_recv.at[step, 0],
            device_id=(a, m, 1 - w),
            device_id_type=MESH,
        )

    def sent_faces(step):
        three_faces(step).wait_send()
        copies = face_copies(step)
        pl.when(m > 0)(copies[3].wait_send)
        pl.when(m < nm - 1)(copies[4].wait_send)

    def traces(step):
        for v in range(NV):
            high, low = halves(adj[v])
            cat[v, 0:64] = high
            cat[v, 64:128] = low
            cat[v, 128:192] = high
            trace[v] = dot(w_trace[...], cat[v])

    def pack(step):
        for v in range(NV):
            sendb[step, 0, v] = tile_of(trace, v, 0, 0)
            sendb[step, 1, v] = tile_of(trace, v, 1, EX - 1)
        copies = face_copies(step)
        copies[0].start()
        copies[1].start()
        for v in range(NV):
            low_y = tile_of(trace, v, 2, 0)
            for ex in range(1, EX):
                low_y = jnp.where(strip == ex, pltpu.roll(tile_of(trace, v, 2, ex), 32 * ex, 1), low_y)
            sendb[step, 3, v] = low_y
            high_y = tile_of(trace, v, 3, EX - 1)
            for ex in range(EX - 1):
                high_y = jnp.where(
                    strip == ex, pltpu.roll(tile_of(trace, v, 3, ex), 32 * (ex + 1), 1), high_y
                )
            sendb[step, 4, v] = high_y
        pl.when(m > 0)(copies[3].start)
        pl.when(m < nm - 1)(copies[4].start)
        for v in range(NV):
            low_z = tile_of(trace, v, 4, 0)
            high_z = pltpu.roll(tile_of(trace, v, 5, 0), 97, 1)
            for ex in range(1, EX):
                low_z = jnp.where(along == ex, pltpu.roll(tile_of(trace, v, 4, ex), ex, 1), low_z)
                high_z = jnp.where(along == ex, pltpu.roll(tile_of(trace, v, 5, ex), 97 + ex, 1), high_z)
            zown[v] = low_z * WALL_SIGN[v]
            sendb[step, 2, v] = jnp.where(w == 0, high_z, low_z)
        copies[2].start()

    def inner_part(step):
        for v in range(NV):
            slopes[v] = dot(w_slope[...], cat[v])

        def chunk(i, carry):
            row = pl.multiple_of((i >> 2) * 16, 16)
            rows = pl.ds(row, 16)
            lanes = pl.ds(pl.multiple_of((i & 3) * TILE, TILE), TILE)
            metric = [met[d, rows, lanes].astype(F32) for d in range(3)]
            slope = []
            for x in range(NV):
                total = metric[0] * slopes[x, rows, lanes]
                for d in range(1, 3):
                    total = total + metric[d] * slopes[x, pl.ds(d * 64 + row, 16), lanes]
                slope.append(total)
            for u in range(NV):
                flux = jac[u, rows, lanes].astype(F32) * slope[0]
                for x in range(1, NV):
                    flux = flux + jac[x * NV + u, rows, lanes].astype(F32) * slope[x]
                base[u, rows, lanes] = adj[u, rows, lanes] + 0.25 * (src[u, rows, lanes] - flux)
            return carry

        lax.fori_loop(0, 16, chunk, 0)

        for v in range(NV):
            for ex in range(EX):
                lanes = slice(ex * TILE, (ex + 1) * TILE)
                parts = (
                    tile_of(trace, v, 1, ex - 1) if ex > 0 else None,
                    tile_of(trace, v, 0, ex + 1) if ex < EX - 1 else None,
                    jnp.where(strip == 0, 0.0, pltpu.roll(tile_of(trace, v, 3, ex), 32, 1)),
                    jnp.where(strip == 3, 0.0, pltpu.roll(tile_of(trace, v, 2, ex), 96, 1)),
                    jnp.where(along == 0, 0.0, pltpu.roll(tile_of(trace, v, 5, ex), 1, 1)),
                    jnp.where(along == 31, 0.0, pltpu.roll(tile_of(trace, v, 4, ex), 127, 1)),
                )
                for side, part in enumerate(parts):
                    rows = slice(side * FPTS, (side + 1) * FPTS)
                    own = tile_of(trace, v, side, ex)
                    jump[v, rows, lanes] = pen[rows, lanes] * (own if part is None else own - part)

    def wait_faces(step):
        three_faces(step).wait_recv()
        copies = face_copies(step)
        pl.when(m > 0)(copies[4].wait_recv)
        pl.when(m < nm - 1)(copies[3].wait_recv)

    def aligned(step, side):
        received = recvb[step, (0, 1, 3, 4)[side]].reshape(NV * FPTS, TILE)
        high, low = halves(received)
        matched = dot(jnp.concatenate([high, low], axis=1), picker[side])
        rows = jnp.concatenate([matched[v * FPTS : (v + 1) * FPTS] for v in range(NV)], axis=1)
        high, low = halves(rows)
        turned = dot(turner, jnp.concatenate([high, low], axis=0))
        code = orient[side : side + 1, :]
        result = []
        for v in range(NV):
            total = jnp.zeros((FPTS, TILE), F32)
            for o in range(8):
                total = jnp.where(
                    code == o, turned[o * FPTS : (o + 1) * FPTS, v * TILE : (v + 1) * TILE], total
                )
            result.append(total)
        return result

    def outer_part(step):
        arrived = [aligned(step, side) for side in range(4)]
        for v in range(NV):
            z_low = jnp.where(w == 0, zown[v], recvb[step, 2, v])
            z_high = jnp.where(w == 0, recvb[step, 2, v], 0.0)
            first = slice(0, TILE)
            last = slice(E - TILE, E)
            jump[v, 0:16, first] = jump[v, 0:16, first] - pen[0:16, first] * arrived[0][v]
            jump[v, 16:32, last] = jump[v, 16:32, last] - pen[16:32, last] * arrived[1][v]
            for ex in range(EX):
                lanes = slice(ex * TILE, (ex + 1) * TILE)
                low_y = arrived[2][v]
                high_y = arrived[3][v]
                low_y = low_y if ex == 0 else pltpu.roll(low_y, TILE - 32 * ex, 1)
                high_y = high_y if ex == EX - 1 else pltpu.roll(high_y, 96 - 32 * ex, 1)
                low_z = z_low if ex == 0 else pltpu.roll(z_low, TILE - ex, 1)
                high_z = pltpu.roll(z_high, 31 - ex, 1)
                edges = (
                    jnp.where(strip == 0, low_y, 0.0),
                    jnp.where(strip == 3, high_y, 0.0),
                    jnp.where(along == 0, low_z, 0.0),
                    jnp.where(along == 31, high_z, 0.0),
                )
                for side, edge in enumerate(edges, start=2):
                    rows = slice(side * FPTS, (side + 1) * FPTS)
                    jump[v, rows, lanes] = jump[v, rows, lanes] - pen[rows, lanes] * edge
            high, low = halves(jump[v])
            jcat[v, 0:96] = high
            jcat[v, 96:192] = low
            lifted = dot(w_lift[...], jcat[v])
            (out if step == STEPS - 1 else adj)[v] = base[v] - 0.25 * (lifted[0:64] + lifted[64:128])

    def plan_routes():
        for side in range(4):
            pick = (iota((TILE, TILE), 0) == match[side : side + 1, :]).astype(F32).astype(BF16)
            picker[side, 0:TILE] = pick
            picker[side, TILE : 2 * TILE] = pick
        count = owner.shape[1]
        block = cells[...] >> 8
        at_block = (iota((count, PTS), 0) == block).astype(F32).astype(BF16)
        owners = jnp.broadcast_to(owner[...].astype(F32), (8, count)).astype(BF16)
        target = dot(owners, at_block)[0:1].astype(I32)
        earlier = (iota((PTS, PTS), 0) < iota((PTS, PTS), 1)).astype(F32).astype(BF16)
        before = dot(at_block, earlier)
        slot = jnp.sum(at_block.astype(F32) * before, axis=0, keepdims=True).astype(I32)
        place = target & (group - 1)
        sector = target >> (group.bit_length() - 1)
        row = iota((8 * group, PTS), 0)
        route_mask[...] = jnp.where(
            ((row >> 3) == place) & ((row & 1) == slot), 1.0, 0.0
        )
        route_to[...] = (iota((TILE, PTS), 0) == sector).astype(F32).astype(BF16)
        offs[...] = (cells[...] & (BLOCK - 1)).astype(F32)
        point = iota((1, PTS), 1) >> 4
        spot = jnp.zeros((1, PTS), I32)
        for n in range(PTS // FPTS):
            face = wall_list[n]
            spot = jnp.where(point == n, (face & 3) * 32 + (face >> 2), spot)
        pick = (iota((TILE, PTS), 0) == spot).astype(F32).astype(BF16)
        spread[0:TILE] = pick
        spread[TILE : 2 * TILE] = pick

    def wall_points():
        wide = iota((NSP, TILE), 1) & 31
        for v in range(NV):
            bottom = out[v, :, 0:TILE]
            for ex in range(1, EX):
                bottom = jnp.where(
                    wide == ex, pltpu.roll(out[v, :, ex * TILE : (ex + 1) * TILE], ex, 1), bottom
                )
            high, low = halves(bottom)
            lanes = slice(v * TILE, (v + 1) * TILE)
            packed[0:64, lanes] = high
            packed[64:128, lanes] = low
            packed[128:192, lanes] = high
        at_wall = dot(w_trace[4 * FPTS : 5 * FPTS], packed[...])
        rows = jnp.concatenate([at_wall[:, v * TILE : (v + 1) * TILE] for v in range(NV)], axis=0)
        high, low = halves(rows)
        expanded = dot(jnp.concatenate([high, low], axis=1), spread[...])
        own_point = (iota((FPTS, PTS), 1) & 15) == iota((FPTS, PTS), 0)
        sens = [jnp.zeros((1, PTS), F32) for c in range(3)]
        for v in range(NV):
            values = jnp.where(own_point, expanded[v * FPTS : (v + 1) * FPTS], 0.0)
            line = jnp.sum(values, axis=0, keepdims=True)
            for c in range(3):
                sens[c] = sens[c] + geom[v, c : c + 1, :].astype(F32) * line
        field = iota((8, PTS), 0) >> 1
        values = jnp.broadcast_to(offs[...], (8, PTS))
        for c in range(3):
            values = jnp.where(field == c, sens[c], values)
        high, low = halves(jnp.concatenate([values] * group, axis=0) * route_mask[...])
        routed = dot_nt(jnp.concatenate([high, low], axis=0), route_to[...])
        routed = routed[0 : 8 * group] + routed[8 * group : 16 * group]
        for g in range(group):
            first_tx[g] = routed[g * 8 : (g + 1) * 8]

    def line_copy(j):
        other = lax.rem(here + j, group)
        return pltpu.make_async_remote_copy(
            src_ref=first_tx.at[other],
            dst_ref=first_rx.at[m],
            send_sem=hop_sem.at[0],
            recv_sem=hop_sem.at[1],
            device_id=(a, other // nw, lax.rem(other, nw)),
            device_id_type=MESH,
        )

    def line_bytes(count):
        return pltpu.make_async_remote_copy(
            src_ref=first_tx.at[0:count],
            dst_ref=first_rx.at[0:count],
            send_sem=hop_sem.at[0],
            recv_sem=hop_sem.at[1],
            device_id=(a, m, 1 - w),
            device_id_type=MESH,
        )

    def ring_copy(j):
        other = lax.rem(a + j, na)
        return pltpu.make_async_remote_copy(
            src_ref=second_tx.at[other],
            dst_ref=second_rx.at[a],
            send_sem=hop_sem.at[2],
            recv_sem=hop_sem.at[3],
            device_id=(other, m, w),
            device_id_type=MESH,
        )

    def ring_bytes():
        return pltpu.make_async_remote_copy(
            src_ref=second_tx.at[0 : na - 1],
            dst_ref=second_rx.at[0 : na - 1],
            send_sem=hop_sem.at[2],
            recv_sem=hop_sem.at[3],
            device_id=(lax.rem(a + 1, na), m, w),
            device_id_type=MESH,
        )

    loaded(0)
    interp_operators()
    loaded(1)
    for step in range(STEPS):
        traces(step)
        if step == 0:
            pl.semaphore_wait(barrier, na - 1 + group - 1)
        else:
            sent_faces(0)
        pack(step)
        if step == 0:
            loaded(2)
            deriv_operators()
            plan_routes()
            loaded(3)
            pen[...] = pen16[...].astype(F32)
        inner_part(step)
        wait_faces(step)
        outer_part(step)

    @pl.when(w == 0)
    def _():
        wall_points()
        for j in range(1, group):
            line_copy(j).start()
        first_rx[m] = first_tx[here]

    @pl.when(w == 0)
    def _():
        line_bytes(nm - 1).wait_recv()

    @pl.when(w != 0)
    def _():
        line_bytes(nm).wait_recv()

    if nm * 8 < TILE:
        second_sq[nm * 8 : TILE] = jnp.zeros((TILE - nm * 8, TILE), F32)
    for source in range(nm):
        second_sq[source * 8 : (source + 1) * 8] = first_rx[source]
    second_sq[...] = second_sq[...].T
    for i in range(na):
        second_tx[i] = second_sq[i : i + 1, :]

    def send_ring(j, carry):
        ring_copy(j).start()
        return carry

    lax.fori_loop(1, na, send_ring, 0)
    second_rx[a] = second_tx[a]
    ring_bytes().wait_recv()
    for i in range(na):
        second_sq[i : i + 1, :] = second_rx[i]
    came = second_sq[0:na, :]
    column = iota((na, BLOCK), 1).astype(F32)
    sums = [jnp.zeros((na, BLOCK), F32) for c in range(3)]
    for source in range(nm):
        for slot in range(2):
            at = source * 8 + slot
            hit = came[:, at + 6 : at + 7] == column
            for c in range(3):
                sums[c] = sums[c] + jnp.where(hit, came[:, at + 2 * c : at + 2 * c + 1], 0.0)
    for c in range(3):
        ffd[c : c + 1, :] = jnp.sum(sums[c], axis=0, keepdims=True)

    sent_faces(STEPS - 1)

    @pl.when(w == 0)
    def _():
        line_bytes(group - 1).wait_send()

    ring_bytes().wait_send()


def solution(mesh):
    sizes = tuple(mesh.shape[name] for name in ("azim", "merid", "wall"))
    na, nm, nw = sizes
    group = nm * nw
    faces = (STEPS, 5, NV, FPTS, TILE)
    scratch = [
        pltpu.VMEM((NV, NSP, E), F32),
        pltpu.VMEM((NV, NSP, E), F32),
        pltpu.VMEM((NV * NV, NSP, E), BF16),
        pltpu.VMEM((3, NSP, E), BF16),
        pltpu.VMEM((NFP, E), BF16),
        pltpu.VMEM((3, NSP, NSP), F32),
        pltpu.VMEM((NSP, NFP), F32),
        pltpu.VMEM((4, TILE), I32),
        pltpu.VMEM((4, TILE), I32),
        pltpu.SMEM((PTS // FPTS,), I32),
        pltpu.VMEM((NV, 3, PTS), BF16),
        pltpu.VMEM((1, PTS), I32),
        pltpu.VMEM((1, na * group), I32),
        pltpu.VMEM((NFP, E), F32),
        pltpu.VMEM((NV, NFP, E), F32),
        pltpu.VMEM((NV, 3 * NSP, E), F32),
        pltpu.VMEM((NV, 3 * NSP, E), BF16),
        pltpu.VMEM((NV, NSP, E), F32),
        pltpu.VMEM((NV, NFP, E), F32),
        pltpu.VMEM((NV, 2 * NFP, E), BF16),
        pltpu.VMEM((NFP, 3 * NSP), BF16),
        pltpu.VMEM((3 * NSP, 3 * NSP), BF16),
        pltpu.VMEM((2 * NSP, 2 * NFP), BF16),
        pltpu.VMEM((TILE, TILE), F32),
        pltpu.VMEM((4, 2 * TILE, TILE), BF16),
        pltpu.VMEM(faces, F32),
        pltpu.VMEM(faces, F32),
        pltpu.VMEM((NV, FPTS, TILE), F32),
        pltpu.VMEM((3 * NSP, NV * TILE), BF16),
        pltpu.VMEM((8 * group, PTS), F32),
        pltpu.VMEM((TILE, PTS), BF16),
        pltpu.VMEM((2 * TILE, PTS), BF16),
        pltpu.VMEM((1, PTS), F32),
        pltpu.VMEM((group, 8, TILE), F32),
        pltpu.VMEM((nm, 8, TILE), F32),
        pltpu.VMEM((TILE, TILE), F32),
        pltpu.VMEM((na, 1, TILE), F32),
        pltpu.VMEM((na, 1, TILE), F32),
        pltpu.SemaphoreType.DMA((4,)),
        pltpu.SemaphoreType.DMA((3,)),
        pltpu.SemaphoreType.DMA((STEPS, 3)),
        pltpu.SemaphoreType.DMA((4,)),
    ]
    hbm = pl.BlockSpec(memory_space=pltpu.HBM)
    vmem = pl.BlockSpec(memory_space=pltpu.VMEM)
    call = pl.pallas_call(
        functools.partial(kernel, sizes),
        out_shape=(pltpu.VMEM((NV, NSP, E), F32), pltpu.VMEM((3, BLOCK), F32)),
        in_specs=[hbm] * 13,
        out_specs=(vmem, vmem),
        scratch_shapes=scratch,
        compiler_params=pltpu.CompilerParams(
            collective_id=0, has_side_effects=True, vmem_limit_bytes=40 * 1024 * 1024
        ),
        name="adjoint_steps",
    )

    def per_device(
        adjoint_in,
        source,
        jacobian,
        metric,
        penalty,
        deriv,
        interp,
        face_match,
        orientation,
        wall_faces,
        wall_geometry,
        lattice_cells,
        block_owner,
    ):
        operands = (
            adjoint_in.reshape(NV, NSP, E),
            source.reshape(NV, NSP, E),
            jacobian.reshape(NV * NV, NSP, E),
            metric.reshape(3, NSP, E),
            penalty.reshape(NFP, E),
            deriv,
            interp.T,
            face_match.reshape(4, TILE),
            orientation.reshape(4, TILE),
            wall_faces.reshape(-1),
            wall_geometry.reshape(3, NV, PTS).transpose(1, 0, 2),
            lattice_cells.reshape(1, PTS),
            block_owner.reshape(1, -1),
        )
        adjoint, owned = call(
            *(pltpu.with_memory_space_constraint(operand, pltpu.HBM) for operand in operands)
        )
        return adjoint[None, None, None], owned

    placed = (
        P("azim", "merid", "wall", None, None, None),
        P("azim", "merid", "wall", None, None, None),
        P("azim", "merid", "wall", None, None, None, None),
        P("azim", "merid", "wall", None, None, None),
        P("azim", "merid", "wall", None, None),
        P(),
        P(),
        P("azim", "merid", "wall", None, None),
        P("azim", "merid", "wall", None, None),
        P("azim", "merid", None),
        P("azim", "merid", None, None, None),
        P("azim", "merid", None),
        P(),
    )
    return jax.shard_map(
        per_device,
        mesh=mesh,
        in_specs=placed,
        out_specs=(
            P("azim", "merid", "wall", None, None, None),
            P(None, ("azim", "merid", "wall")),
        ),
        check_vma=False,
    )
```

```python
import functools

import jax
import jax.numpy as jnp
from jax import lax
from jax.experimental import pallas as pl
from jax.experimental.pallas import tpu as pltpu
from jax.sharding import PartitionSpec as P

MESH = pl.DeviceIdType.MESH
F32, BF16, I32 = jnp.float32, jnp.bfloat16, jnp.int32

NV = 5
NSP = 64
FPTS = 16
NFP = 96
EX = 4
E = 512
PTS = 256
STEPS = 2
BLOCK = 256
TILE = 128
WALL_SIGN = (1.0, 1.0, 1.0, -1.0, 1.0)


def iota(shape, axis):
    return lax.broadcasted_iota(I32, shape, axis)


def halves(value):
    high = value.astype(BF16)
    low = (value - high.astype(F32)).astype(BF16)
    return high, low


def dot(left, right):
    return jnp.dot(left, right, preferred_element_type=F32)


def dot_nt(left, right):
    return lax.dot_general(left, right, (((1,), (1,)), ((), ())), preferred_element_type=F32)


def rounds(count):
    def offsets(steps):
        return tuple(sorted({step % count for step in steps} - {0}))

    near, second, third = offsets((1, -1, 2, -2, 8, -8)), offsets((2, -2, 8, -8)), offsets((4, -4, 16))
    one = {0, *near}
    two = one | {(i + j) % count for i in one for j in second}
    all_known = two | {(i + j) % count for i in two for j in third}
    if len(all_known) == count and set(second) <= one and set(third) <= two:
        return near, second, third
    return offsets(range(count)), (), ()


def turn_rows():
    row = iota((8 * FPTS, 2 * FPTS), 0)
    col = iota((8 * FPTS, 2 * FPTS), 1) & (FPTS - 1)
    code, point = row >> 4, row & 15
    i, k = point >> 2, point & 3
    first = jnp.where((code & 4) != 0, k, i)
    second = jnp.where((code & 4) != 0, i, k)
    first = jnp.where((code & 1) != 0, 3 - first, first)
    second = jnp.where((code & 2) != 0, 3 - second, second)
    return (first * 4 + second == col).astype(F32).astype(BF16)


def tile_of(ref, v, side, ex):
    return ref[v, side * FPTS : (side + 1) * FPTS, ex * TILE : (ex + 1) * TILE]


def kernel(
    sizes,
    adj_hbm,
    src_hbm,
    jac_hbm,
    met_hbm,
    pen_hbm,
    deriv_hbm,
    interp_hbm,
    match_hbm,
    orient_hbm,
    list_hbm,
    geom_hbm,
    cells_hbm,
    owner_hbm,
    out,
    ffd,
    adj,
    src,
    jac,
    met,
    pen16,
    deriv,
    interp_t,
    match,
    orient,
    wall_list,
    geom,
    cells,
    owner,
    pen,
    trace,
    slopes,
    cat,
    base,
    jump,
    jcat,
    w_trace,
    w_slope,
    w_lift,
    w_pair,
    ahead,
    arrived,
    pen_low,
    wall_ahead,
    square,
    picker,
    sendb,
    recvb,
    zown,
    packed,
    route_mask,
    route_to,
    spread,
    offs,
    first_tx,
    first_rx,
    second_sq,
    second_tx,
    second_rx,
    load_sem,
    face_send,
    face_recv,
    hop_sem,
    told,
):
    na, nm, nw = sizes
    group = nm * nw
    a, m, w = lax.axis_index("azim"), lax.axis_index("merid"), lax.axis_index("wall")
    here = m * nw + w

    groups = (
        ((interp_hbm, interp_t),),
        ((adj_hbm, adj),),
        (
            (deriv_hbm, deriv),
            (match_hbm, match),
            (cells_hbm, cells),
            (owner_hbm, owner),
            (list_hbm, wall_list),
        ),
        (
            (pen_hbm, pen16),
            (met_hbm, met),
            (jac_hbm, jac),
            (src_hbm, src),
            (orient_hbm, orient),
            (geom_hbm, geom),
        ),
    )
    loads = [
        [pltpu.make_async_copy(*pair, load_sem.at[i]) for pair in group_here]
        for i, group_here in enumerate(groups)
    ]
    for part in loads[:2]:
        for load in part:
            load.start()

    def loaded(part):
        for load in loads[part]:
            load.wait()

    near, second, third = rounds(na)
    barrier = pltpu.get_barrier_semaphore()

    def sector(offset):
        return lax.rem(a + offset, na), m, w

    for offset in near:
        pl.semaphore_signal(barrier, inc=1, device_id=sector(offset), device_id_type=MESH)
    for j in range(1, group):
        other = lax.rem(here + j, group)
        pl.semaphore_signal(
            barrier, inc=1, device_id=(a, other // nw, lax.rem(other, nw)), device_id_type=MESH
        )
    for part in loads[2:]:
        for load in part:
            load.start()

    def tell(at, offsets):
        for offset in offsets:
            pl.semaphore_signal(
                told.at[at], inc=1, device_id=sector(offset), device_id_type=MESH
            )

    def hear(at, offsets):
        if offsets:
            pl.semaphore_wait(told.at[at], len(offsets))

    for end, side in ((0, 3), (nm - 1, 4)):

        @pl.when(m == end)
        def _():
            for step in range(STEPS):
                recvb[step, side] = jnp.zeros((NV, FPTS, TILE), F32)

    lane = iota((FPTS, TILE), 1)
    strip = lane >> 5
    along = lane & 31
    turner = turn_rows()

    def interp_operators():
        square[0:64, 0:96] = interp_t[...]
        high, low = halves(square[...].T[0:96, 0:64])
        w_trace[:, 0:64] = high
        w_trace[:, 64:128] = high
        w_trace[:, 128:192] = low
        high, low = halves(interp_t[...])
        w_lift[0:64, 0:96] = high
        w_lift[0:64, 96:192] = high
        w_lift[64:128, 0:96] = low
        w_lift[64:128, 96:192] = low

    def pair_operators():
        pair = dot(w_trace[...], jnp.concatenate([*halves(interp_t[...]), halves(interp_t[...])[0]], axis=0))
        high, low = halves(pair)
        w_pair[0:96, 0:96] = high
        w_pair[0:96, 96:192] = high
        w_pair[96:192, 0:96] = low
        w_pair[96:192, 96:192] = low

    def deriv_operators():
        for d in range(3):
            square[0:64, 0:64] = deriv[d]
            high, low = halves(square[...].T[0:64, 0:64])
            w_slope[d * 64 : (d + 1) * 64, 0:64] = high
            w_slope[d * 64 : (d + 1) * 64, 64:128] = high
            w_slope[d * 64 : (d + 1) * 64, 128:192] = low

    def face_copy(step, at, side, target):
        return pltpu.make_async_remote_copy(
            src_ref=sendb.at[step, at],
            dst_ref=recvb.at[step, side],
            send_sem=face_send.at[max(at - 2, 0)],
            recv_sem=face_recv.at[step, max(side - 2, 0)],
            device_id=target,
            device_id_type=MESH,
        )

    def face_copies(step):
        return (
            face_copy(step, 0, 1, (lax.rem(a + na - 1, na), m, w)),
            face_copy(step, 1, 0, (lax.rem(a + 1, na), m, w)),
            face_copy(step, 2, 2, (a, m, 1 - w)),
            face_copy(step, 3, 4, (a, jnp.maximum(m - 1, 0), w)),
            face_copy(step, 4, 3, (a, jnp.minimum(m + 1, nm - 1), w)),
        )

    def three_faces(step):
        return pltpu.make_async_remote_copy(
            src_ref=sendb.at[step, 0:3],
            dst_ref=recvb.at[step, 0:3],
            send_sem=face_send.at[0],
            recv_sem=face_recv.at[step, 0],
            device_id=(a, m, 1 - w),
            device_id_type=MESH,
        )

    def sent_faces(step):
        three_faces(step).wait_send()
        copies = face_copies(step)
        pl.when(m > 0)(copies[3].wait_send)
        pl.when(m < nm - 1)(copies[4].wait_send)

    def split(v, value):
        high, low = halves(value)
        cat[v, 0:64] = high
        cat[v, 64:128] = low
        cat[v, 128:192] = high

    def first_traces():
        for v in range(NV):
            split(v, adj[v])
            trace[v] = dot(w_trace[...], cat[v])

    def later_traces():
        for v in range(NV):
            added = dot(w_pair[...], jcat[v])
            trace[v] = ahead[v] - 0.25 * (added[0:96] + added[96:192])

    def update(v, target):
        lifted = dot(w_lift[...], jcat[v])
        target[v] = base[v] - 0.25 * (lifted[0:64] + lifted[64:128])

    def bottom_of(ref, v, row):
        rows = slice(row, row + FPTS)
        value = ref[v, rows, 0:TILE]
        for ex in range(1, EX):
            value = jnp.where(
                along == ex, pltpu.roll(ref[v, rows, ex * TILE : (ex + 1) * TILE], ex, 1), value
            )
        return value

    def pack(step):
        for v in range(NV):
            sendb[step, 0, v] = tile_of(trace, v, 0, 0)
            sendb[step, 1, v] = tile_of(trace, v, 1, EX - 1)
        copies = face_copies(step)
        copies[0].start()
        copies[1].start()
        for v in range(NV):
            low_y = tile_of(trace, v, 2, 0)
            for ex in range(1, EX):
                low_y = jnp.where(strip == ex, pltpu.roll(tile_of(trace, v, 2, ex), 32 * ex, 1), low_y)
            sendb[step, 3, v] = low_y
            high_y = tile_of(trace, v, 3, EX - 1)
            for ex in range(EX - 1):
                high_y = jnp.where(
                    strip == ex, pltpu.roll(tile_of(trace, v, 3, ex), 32 * (ex + 1), 1), high_y
                )
            sendb[step, 4, v] = high_y
        pl.when(m > 0)(copies[3].start)
        pl.when(m < nm - 1)(copies[4].start)
        for v in range(NV):
            low_z = tile_of(trace, v, 4, 0)
            high_z = pltpu.roll(tile_of(trace, v, 5, 0), 97, 1)
            for ex in range(1, EX):
                low_z = jnp.where(along == ex, pltpu.roll(tile_of(trace, v, 4, ex), ex, 1), low_z)
                high_z = jnp.where(along == ex, pltpu.roll(tile_of(trace, v, 5, ex), 97 + ex, 1), high_z)
            zown[v] = low_z * WALL_SIGN[v]
            sendb[step, 2, v] = jnp.where(w == 0, high_z, low_z)
        copies[2].start()

    def inner_part(step):
        for v in range(NV):
            if step > 0:
                update(v, adj)
                split(v, adj[v])
            slopes[v] = dot(w_slope[...], cat[v])

        def chunk(i, carry):
            row = pl.multiple_of((i >> 2) * 16, 16)
            rows = pl.ds(row, 16)
            lanes = pl.ds(pl.multiple_of((i & 3) * TILE, TILE), TILE)
            metric = [met[d, rows, lanes].astype(F32) for d in range(3)]
            slope = []
            for x in range(NV):
                total = metric[0] * slopes[x, rows, lanes]
                for d in range(1, 3):
                    total = total + metric[d] * slopes[x, pl.ds(d * 64 + row, 16), lanes]
                slope.append(total)
            for u in range(NV):
                flux = jac[u, rows, lanes].astype(F32) * slope[0]
                for x in range(1, NV):
                    flux = flux + jac[x * NV + u, rows, lanes].astype(F32) * slope[x]
                base[u, rows, lanes] = adj[u, rows, lanes] + 0.25 * (src[u, rows, lanes] - flux)
            return carry

        lax.fori_loop(0, 16, chunk, 0)
        if step < STEPS - 1:
            for v in range(NV):
                split(v, base[v])
                ahead[v] = dot(w_trace[...], cat[v])

        for v in range(NV):
            for ex in range(EX):
                lanes = slice(ex * TILE, (ex + 1) * TILE)
                parts = (
                    tile_of(trace, v, 1, ex - 1) if ex > 0 else None,
                    tile_of(trace, v, 0, ex + 1) if ex < EX - 1 else None,
                    jnp.where(strip == 0, 0.0, pltpu.roll(tile_of(trace, v, 3, ex), 32, 1)),
                    jnp.where(strip == 3, 0.0, pltpu.roll(tile_of(trace, v, 2, ex), 96, 1)),
                    jnp.where(along == 0, 0.0, pltpu.roll(tile_of(trace, v, 5, ex), 1, 1)),
                    jnp.where(along == 31, 0.0, pltpu.roll(tile_of(trace, v, 4, ex), 127, 1)),
                )
                for side, part in enumerate(parts):
                    rows = slice(side * FPTS, (side + 1) * FPTS)
                    own = tile_of(trace, v, side, ex)
                    jump[v, rows, lanes] = pen[rows, lanes] * (own if part is None else own - part)

    def wait_faces(step):
        three_faces(step).wait_recv()
        copies = face_copies(step)
        pl.when(m > 0)(copies[4].wait_recv)
        pl.when(m < nm - 1)(copies[3].wait_recv)

    def align(step):
        for side in range(4):
            received = recvb[step, (0, 1, 3, 4)[side]].reshape(NV * FPTS, TILE)
            high, low = halves(received)
            matched = dot(jnp.concatenate([high, low], axis=1), picker[side])
            rows = jnp.concatenate(
                [matched[v * FPTS : (v + 1) * FPTS] for v in range(NV)], axis=1
            )
            high, low = halves(rows)
            turned = dot(turner, jnp.concatenate([high, low], axis=0))
            code = orient[side : side + 1, :]
            for v in range(NV):
                total = jnp.zeros((FPTS, TILE), F32)
                for o in range(8):
                    total = jnp.where(
                        code == o,
                        turned[o * FPTS : (o + 1) * FPTS, v * TILE : (v + 1) * TILE],
                        total,
                    )
                arrived[side, v] = total

    def outer_part(step):
        for v in range(NV):
            z_low = jnp.where(w == 0, zown[v], recvb[step, 2, v])
            z_high = jnp.where(w == 0, recvb[step, 2, v], 0.0)
            first = slice(0, TILE)
            last = slice(E - TILE, E)
            jump[v, 0:16, first] = jump[v, 0:16, first] - pen[0:16, first] * arrived[0, v]
            jump[v, 16:32, last] = jump[v, 16:32, last] - pen[16:32, last] * arrived[1, v]
            for ex in range(EX):
                lanes = slice(ex * TILE, (ex + 1) * TILE)
                low_y = arrived[2, v]
                high_y = arrived[3, v]
                low_y = low_y if ex == 0 else pltpu.roll(low_y, TILE - 32 * ex, 1)
                high_y = high_y if ex == EX - 1 else pltpu.roll(high_y, 96 - 32 * ex, 1)
                low_z = z_low if ex == 0 else pltpu.roll(z_low, TILE - ex, 1)
                high_z = pltpu.roll(z_high, 31 - ex, 1)
                edges = (
                    jnp.where(strip == 0, low_y, 0.0),
                    jnp.where(strip == 3, high_y, 0.0),
                    jnp.where(along == 0, low_z, 0.0),
                    jnp.where(along == 31, high_z, 0.0),
                )
                for side, edge in enumerate(edges, start=2):
                    rows = slice(side * FPTS, (side + 1) * FPTS)
                    jump[v, rows, lanes] = jump[v, rows, lanes] - pen[rows, lanes] * edge
            high, low = halves(jump[v])
            jcat[v, 0:96] = high
            jcat[v, 96:192] = low

    def plan_routes():
        for side in range(4):
            pick = (iota((TILE, TILE), 0) == match[side : side + 1, :]).astype(F32).astype(BF16)
            picker[side, 0:TILE] = pick
            picker[side, TILE : 2 * TILE] = pick
        count = owner.shape[1]
        block = cells[...] >> 8
        at_block = (iota((count, PTS), 0) == block).astype(F32).astype(BF16)
        owners = jnp.broadcast_to(owner[...].astype(F32), (8, count)).astype(BF16)
        target = dot(owners, at_block)[0:1].astype(I32)
        earlier = (iota((PTS, PTS), 0) < iota((PTS, PTS), 1)).astype(F32).astype(BF16)
        before = dot(at_block, earlier)
        slot = jnp.sum(at_block.astype(F32) * before, axis=0, keepdims=True).astype(I32)
        place = target & (group - 1)
        sector = target >> (group.bit_length() - 1)
        row = iota((8 * group, PTS), 0)
        route_mask[...] = jnp.where(
            ((row >> 3) == place) & ((row & 1) == slot), 1.0, 0.0
        )
        route_to[...] = (iota((TILE, PTS), 0) == sector).astype(F32).astype(BF16)
        offs[...] = (cells[...] & (BLOCK - 1)).astype(F32)
        point = iota((1, PTS), 1) >> 4
        spot = jnp.zeros((1, PTS), I32)
        for n in range(PTS // FPTS):
            face = wall_list[n]
            spot = jnp.where(point == n, (face & 3) * 32 + (face >> 2), spot)
        pick = (iota((TILE, PTS), 0) == spot).astype(F32).astype(BF16)
        spread[0:TILE] = pick
        spread[TILE : 2 * TILE] = pick

    def at_z_low(values):
        added = dot(jnp.concatenate([w_pair[64:80], w_pair[160:176]], axis=0), values)
        return 0.25 * (added[0:16] + added[16:32])

    def bottom_ahead():
        for side in range(5):
            rows = slice(side * FPTS, (side + 1) * FPTS)
            value = pen[rows, 0:TILE]
            for ex in range(1, EX):
                value = jnp.where(
                    along == ex, pltpu.roll(pen[rows, ex * TILE : (ex + 1) * TILE], ex, 1), value
                )
            pen_low[rows] = value
        for v in range(NV):
            lanes = slice(v * TILE, (v + 1) * TILE)
            for part in range(4):
                rows = slice(part * FPTS, (part + 1) * FPTS)
                high, low = halves(bottom_of(base, v, part * FPTS))
                packed[rows, lanes] = high
                packed[64 + part * FPTS : 80 + part * FPTS, lanes] = low
                packed[128 + part * FPTS : 144 + part * FPTS, lanes] = high
        wall_ahead[...] = dot(w_trace[64:80], packed[...])
        for v in range(NV):
            lanes = slice(v * TILE, (v + 1) * TILE)
            for side in range(6):
                high, low = halves(bottom_of(jump, v, side * FPTS))
                packed[side * FPTS : (side + 1) * FPTS, lanes] = high
                packed[96 + side * FPTS : 112 + side * FPTS, lanes] = low
        wall_ahead[...] = wall_ahead[...] - at_z_low(packed[...])
        packed[80:96] = jnp.zeros((FPTS, NV * TILE), BF16)
        packed[176:192] = jnp.zeros((FPTS, NV * TILE), BF16)

    def wall_points():
        for v in range(NV):
            lanes = slice(v * TILE, (v + 1) * TILE)
            low_y = jnp.zeros((FPTS, TILE), F32)
            high_y = jnp.zeros((FPTS, TILE), F32)
            for ex in range(EX):
                from_low = arrived[2, v] if ex == 0 else pltpu.roll(arrived[2, v], TILE - 31 * ex, 1)
                low_y = jnp.where(lane == ex, from_low, low_y)
                from_high = pltpu.roll(arrived[3, v], 96 - 31 * ex, 1)
                high_y = jnp.where(lane == 96 + ex, from_high, high_y)
            edges = (
                jnp.where(along == 0, arrived[0, v], 0.0),
                jnp.where(along == EX - 1, pltpu.roll(arrived[1, v], EX - 1, 1), 0.0),
                low_y,
                high_y,
                zown[v],
            )
            for side, edge in enumerate(edges):
                rows = slice(side * FPTS, (side + 1) * FPTS)
                high, low = halves(pen_low[rows] * edge)
                packed[rows, lanes] = high
                packed[96 + side * FPTS : 112 + side * FPTS, lanes] = low
        at_wall = wall_ahead[...] + at_z_low(packed[...])
        rows = jnp.concatenate([at_wall[:, v * TILE : (v + 1) * TILE] for v in range(NV)], axis=0)
        high, low = halves(rows)
        expanded = dot(jnp.concatenate([high, low], axis=1), spread[...])
        own_point = (iota((FPTS, PTS), 1) & 15) == iota((FPTS, PTS), 0)
        sens = [jnp.zeros((1, PTS), F32) for c in range(3)]
        for v in range(NV):
            values = jnp.where(own_point, expanded[v * FPTS : (v + 1) * FPTS], 0.0)
            line = jnp.sum(values, axis=0, keepdims=True)
            for c in range(3):
                sens[c] = sens[c] + geom[v, c : c + 1, :].astype(F32) * line
        field = iota((8, PTS), 0) >> 1
        values = jnp.broadcast_to(offs[...], (8, PTS))
        for c in range(3):
            values = jnp.where(field == c, sens[c], values)
        high, low = halves(jnp.concatenate([values] * group, axis=0) * route_mask[...])
        routed = dot_nt(jnp.concatenate([high, low], axis=0), route_to[...])
        routed = routed[0 : 8 * group] + routed[8 * group : 16 * group]
        for g in range(group):
            first_tx[g] = routed[g * 8 : (g + 1) * 8]

    def line_copy(j):
        other = lax.rem(here + j, group)
        return pltpu.make_async_remote_copy(
            src_ref=first_tx.at[other],
            dst_ref=first_rx.at[m],
            send_sem=hop_sem.at[0],
            recv_sem=hop_sem.at[1],
            device_id=(a, other // nw, lax.rem(other, nw)),
            device_id_type=MESH,
        )

    def line_bytes(count):
        return pltpu.make_async_remote_copy(
            src_ref=first_tx.at[0:count],
            dst_ref=first_tx.at[0:count],
            send_sem=hop_sem.at[0],
            recv_sem=hop_sem.at[1],
            device_id=(a, m, 1 - w),
            device_id_type=MESH,
        )

    def ring_copy(j):
        other = lax.rem(a + j, na)
        return pltpu.make_async_remote_copy(
            src_ref=second_tx.at[other],
            dst_ref=second_rx.at[a],
            send_sem=hop_sem.at[2],
            recv_sem=hop_sem.at[3],
            device_id=(other, m, w),
            device_id_type=MESH,
        )

    def ring_bytes():
        return pltpu.make_async_remote_copy(
            src_ref=second_tx.at[0 : na - 1],
            dst_ref=second_rx.at[0 : na - 1],
            send_sem=hop_sem.at[2],
            recv_sem=hop_sem.at[3],
            device_id=(lax.rem(a + 1, na), m, w),
            device_id_type=MESH,
        )

    loaded(0)
    interp_operators()
    loaded(1)
    first_traces()
    pl.semaphore_wait(barrier, len(near) + group - 1)
    pack(0)
    tell(0, second)
    loaded(2)
    pair_operators()
    deriv_operators()
    plan_routes()
    loaded(3)
    pen[...] = pen16[...].astype(F32)
    inner_part(0)
    wait_faces(0)
    hear(0, second)
    tell(1, third)
    align(0)
    outer_part(0)
    later_traces()
    sent_faces(0)
    pack(1)
    inner_part(1)

    @pl.when(w == 0)
    def _():
        bottom_ahead()

    wait_faces(1)
    hear(1, third)
    align(1)

    @pl.when(w == 0)
    def _():
        wall_points()
        for j in range(1, group):
            line_copy(j).start()
        first_rx[m] = first_tx[here]

    outer_part(1)
    for v in range(NV):
        update(v, out)

    @pl.when(w == 0)
    def _():
        line_bytes(nm - 1).wait_recv()

    @pl.when(w != 0)
    def _():
        line_bytes(nm).wait_recv()

    if nm * 8 < TILE:
        second_sq[nm * 8 : TILE] = jnp.zeros((TILE - nm * 8, TILE), F32)
    for source in range(nm):
        second_sq[source * 8 : (source + 1) * 8] = first_rx[source]
    second_sq[...] = second_sq[...].T
    for i in range(na):
        second_tx[i] = second_sq[i : i + 1, :]

    def send_ring(j, carry):
        ring_copy(j).start()
        return carry

    lax.fori_loop(1, na, send_ring, 0)
    second_rx[a] = second_tx[a]
    ring_bytes().wait_recv()
    for i in range(na):
        second_sq[i : i + 1, :] = second_rx[i]
    came = second_sq[0:na, :]
    column = iota((na, BLOCK), 1).astype(F32)
    sums = [jnp.zeros((na, BLOCK), F32) for c in range(3)]
    for source in range(nm):
        for slot in range(2):
            at = source * 8 + slot
            hit = came[:, at + 6 : at + 7] == column
            for c in range(3):
                sums[c] = sums[c] + jnp.where(hit, came[:, at + 2 * c : at + 2 * c + 1], 0.0)
    for c in range(3):
        ffd[c : c + 1, :] = jnp.sum(sums[c], axis=0, keepdims=True)

    sent_faces(STEPS - 1)

    @pl.when(w == 0)
    def _():
        line_bytes(group - 1).wait_send()

    ring_bytes().wait_send()


def solution(mesh):
    sizes = tuple(mesh.shape[name] for name in ("azim", "merid", "wall"))
    na, nm, nw = sizes
    group = nm * nw
    faces = (STEPS, 5, NV, FPTS, TILE)
    scratch = [
        pltpu.VMEM((NV, NSP, E), F32),
        pltpu.VMEM((NV, NSP, E), F32),
        pltpu.VMEM((NV * NV, NSP, E), BF16),
        pltpu.VMEM((3, NSP, E), BF16),
        pltpu.VMEM((NFP, E), BF16),
        pltpu.VMEM((3, NSP, NSP), F32),
        pltpu.VMEM((NSP, NFP), F32),
        pltpu.VMEM((4, TILE), I32),
        pltpu.VMEM((4, TILE), I32),
        pltpu.SMEM((PTS // FPTS,), I32),
        pltpu.VMEM((NV, 3, PTS), BF16),
        pltpu.VMEM((1, PTS), I32),
        pltpu.VMEM((1, na * group), I32),
        pltpu.VMEM((NFP, E), F32),
        pltpu.VMEM((NV, NFP, E), F32),
        pltpu.VMEM((NV, 3 * NSP, E), F32),
        pltpu.VMEM((NV, 3 * NSP, E), BF16),
        pltpu.VMEM((NV, NSP, E), F32),
        pltpu.VMEM((NV, NFP, E), F32),
        pltpu.VMEM((NV, 2 * NFP, E), BF16),
        pltpu.VMEM((NFP, 3 * NSP), BF16),
        pltpu.VMEM((3 * NSP, 3 * NSP), BF16),
        pltpu.VMEM((2 * NSP, 2 * NFP), BF16),
        pltpu.VMEM((2 * NFP, 2 * NFP), BF16),
        pltpu.VMEM((NV, NFP, E), F32),
        pltpu.VMEM((4, NV, FPTS, TILE), F32),
        pltpu.VMEM((5 * FPTS, TILE), F32),
        pltpu.VMEM((FPTS, NV * TILE), F32),
        pltpu.VMEM((TILE, TILE), F32),
        pltpu.VMEM((4, 2 * TILE, TILE), BF16),
        pltpu.VMEM(faces, F32),
        pltpu.VMEM(faces, F32),
        pltpu.VMEM((NV, FPTS, TILE), F32),
        pltpu.VMEM((3 * NSP, NV * TILE), BF16),
        pltpu.VMEM((8 * group, PTS), F32),
        pltpu.VMEM((TILE, PTS), BF16),
        pltpu.VMEM((2 * TILE, PTS), BF16),
        pltpu.VMEM((1, PTS), F32),
        pltpu.VMEM((group, 8, TILE), F32),
        pltpu.VMEM((nm, 8, TILE), F32),
        pltpu.VMEM((TILE, TILE), F32),
        pltpu.VMEM((na, 1, TILE), F32),
        pltpu.VMEM((na, 1, TILE), F32),
        pltpu.SemaphoreType.DMA((4,)),
        pltpu.SemaphoreType.DMA((3,)),
        pltpu.SemaphoreType.DMA((STEPS, 3)),
        pltpu.SemaphoreType.DMA((4,)),
        pltpu.SemaphoreType.REGULAR((2,)),
    ]
    hbm = pl.BlockSpec(memory_space=pltpu.HBM)
    vmem = pl.BlockSpec(memory_space=pltpu.VMEM)
    call = pl.pallas_call(
        functools.partial(kernel, sizes),
        out_shape=(pltpu.VMEM((NV, NSP, E), F32), pltpu.VMEM((3, BLOCK), F32)),
        in_specs=[hbm] * 13,
        out_specs=(vmem, vmem),
        scratch_shapes=scratch,
        compiler_params=pltpu.CompilerParams(
            collective_id=0, has_side_effects=True, vmem_limit_bytes=40 * 1024 * 1024
        ),
        name="adjoint_steps",
    )

    def per_device(
        adjoint_in,
        source,
        jacobian,
        metric,
        penalty,
        deriv,
        interp,
        face_match,
        orientation,
        wall_faces,
        wall_geometry,
        lattice_cells,
        block_owner,
    ):
        operands = (
            adjoint_in.reshape(NV, NSP, E),
            source.reshape(NV, NSP, E),
            jacobian.reshape(NV * NV, NSP, E),
            metric.reshape(3, NSP, E),
            penalty.reshape(NFP, E),
            deriv,
            interp.T,
            face_match.reshape(4, TILE),
            orientation.reshape(4, TILE),
            wall_faces.reshape(-1),
            wall_geometry.reshape(3, NV, PTS).transpose(1, 0, 2),
            lattice_cells.reshape(1, PTS),
            block_owner.reshape(1, -1),
        )
        adjoint, owned = call(
            *(pltpu.with_memory_space_constraint(operand, pltpu.HBM) for operand in operands)
        )
        return adjoint[None, None, None], owned

    placed = (
        P("azim", "merid", "wall", None, None, None),
        P("azim", "merid", "wall", None, None, None),
        P("azim", "merid", "wall", None, None, None, None),
        P("azim", "merid", "wall", None, None, None),
        P("azim", "merid", "wall", None, None),
        P(),
        P(),
        P("azim", "merid", "wall", None, None),
        P("azim", "merid", "wall", None, None),
        P("azim", "merid", None),
        P("azim", "merid", None, None, None),
        P("azim", "merid", None),
        P(),
    )
    return jax.shard_map(
        per_device,
        mesh=mesh,
        in_specs=placed,
        out_specs=(
            P("azim", "merid", "wall", None, None, None),
            P(None, ("azim", "merid", "wall")),
        ),
        check_vma=False,
    )
```

```python
import functools

import jax
import jax.numpy as jnp
from jax import lax
from jax.experimental import pallas as pl
from jax.experimental.pallas import tpu as pltpu
from jax.sharding import PartitionSpec as P

MESH = pl.DeviceIdType.MESH
F32, BF16, I32 = jnp.float32, jnp.bfloat16, jnp.int32

NV = 5
NSP = 64
FPTS = 16
NFP = 96
EX = 4
E = 512
PTS = 256
STEPS = 2
BLOCK = 256
TILE = 128
WALL_SIGN = (1.0, 1.0, 1.0, -1.0, 1.0)


def iota(shape, axis):
    return lax.broadcasted_iota(I32, shape, axis)


def halves(value):
    high = value.astype(BF16)
    low = (value - high.astype(F32)).astype(BF16)
    return high, low


def dot(left, right):
    return jnp.dot(left, right, preferred_element_type=F32)


def dot_nt(left, right):
    return lax.dot_general(left, right, (((1,), (1,)), ((), ())), preferred_element_type=F32)


def rounds(count):
    def offsets(steps):
        return tuple(sorted({step % count for step in steps} - {0}))

    near, second, third = offsets((1, -1, 2, -2, 8, -8)), offsets((2, -2, 8, -8)), offsets((4, -4, 16))
    one = {0, *near}
    two = one | {(i + j) % count for i in one for j in second}
    all_known = two | {(i + j) % count for i in two for j in third}
    if len(all_known) == count and set(second) <= one and set(third) <= two:
        return near, second, third
    return offsets(range(count)), (), ()


def far_first(count):
    def hops(offset):
        y, z = divmod(offset, 8)
        return min(y, 4 - y) + min(z, 8 - z)

    return sorted(range(count), key=hops, reverse=True)


def turned_points(code):
    row = iota((FPTS, TILE), 0)
    i, k = row >> 2, row & 3
    first = jnp.where((code & 4) != 0, k, i)
    second = jnp.where((code & 4) != 0, i, k)
    first = jnp.where((code & 1) != 0, 3 - first, first)
    second = jnp.where((code & 2) != 0, 3 - second, second)
    return first * 4 + second


def tile_of(ref, v, side, ex):
    return ref[v, side * FPTS : (side + 1) * FPTS, ex * TILE : (ex + 1) * TILE]


def kernel(
    sizes,
    adj_hbm,
    src_hbm,
    jac_hbm,
    met_hbm,
    pen_hbm,
    deriv_hbm,
    interp_hbm,
    match_hbm,
    orient_hbm,
    list_hbm,
    geom_hbm,
    cells_hbm,
    owner_hbm,
    out,
    ffd,
    adj,
    src,
    jac,
    met,
    pen16,
    deriv,
    interp_t,
    match,
    orient,
    wall_list,
    geom,
    cells,
    owner,
    pen,
    trace,
    slopes,
    cat,
    base,
    jump,
    jcat,
    w_trace,
    w_slope,
    w_lift,
    w_pair,
    ahead,
    arrived,
    pen_low,
    wall_ahead,
    square,
    turn,
    sendb,
    recvb,
    zown,
    packed,
    slot_mask,
    to_owner,
    spread,
    offs,
    message,
    goes,
    came,
    load_sem,
    face_send,
    face_recv,
    hop_sem,
    told,
):
    na, nm, nw = sizes
    group = nm * nw
    a, m, w = lax.axis_index("azim"), lax.axis_index("merid"), lax.axis_index("wall")
    here = m * nw + w

    groups = (
        ((interp_hbm, interp_t),),
        ((adj_hbm, adj),),
        (
            (deriv_hbm, deriv),
            (match_hbm, match),
            (cells_hbm, cells),
            (owner_hbm, owner),
            (list_hbm, wall_list),
            (orient_hbm, orient),
        ),
        (
            (pen_hbm, pen16),
            (met_hbm, met),
            (jac_hbm, jac),
            (src_hbm, src),
            (geom_hbm, geom),
        ),
    )
    loads = [
        [pltpu.make_async_copy(*pair, load_sem.at[i]) for pair in group_here]
        for i, group_here in enumerate(groups)
    ]
    for part in loads[:2]:
        for load in part:
            load.start()

    def loaded(part):
        for load in loads[part]:
            load.wait()

    near, second, third = rounds(na)
    barrier = pltpu.get_barrier_semaphore()

    def sector(offset):
        return lax.rem(a + offset, na), m, w

    for offset in near:
        pl.semaphore_signal(barrier, inc=1, device_id=sector(offset), device_id_type=MESH)
    for j in range(1, group):
        other = lax.rem(here + j, group)
        pl.semaphore_signal(
            barrier, inc=1, device_id=(a, other // nw, lax.rem(other, nw)), device_id_type=MESH
        )
    for part in loads[2:]:
        for load in part:
            load.start()

    def tell(at, offsets):
        for offset in offsets:
            pl.semaphore_signal(
                told.at[at], inc=1, device_id=sector(offset), device_id_type=MESH
            )

    def hear(at, offsets):
        if offsets:
            pl.semaphore_wait(told.at[at], len(offsets))

    for end, side in ((0, 3), (nm - 1, 4)):

        @pl.when(m == end)
        def _():
            for step in range(STEPS):
                recvb[step, side] = jnp.zeros((NV, FPTS, TILE), F32)

    lane = iota((FPTS, TILE), 1)
    strip = lane >> 5
    along = lane & 31

    def interp_operators():
        square[0:64, 0:96] = interp_t[...]
        high, low = halves(square[...].T[0:96, 0:64])
        w_trace[:, 0:64] = high
        w_trace[:, 64:128] = high
        w_trace[:, 128:192] = low
        high, low = halves(interp_t[...])
        w_lift[0:64, 0:96] = high
        w_lift[0:64, 96:192] = high
        w_lift[64:128, 0:96] = low
        w_lift[64:128, 96:192] = low

    def pair_operators():
        pair = dot(w_trace[...], jnp.concatenate([*halves(interp_t[...]), halves(interp_t[...])[0]], axis=0))
        high, low = halves(pair)
        w_pair[0:96, 0:96] = high
        w_pair[0:96, 96:192] = high
        w_pair[96:192, 0:96] = low
        w_pair[96:192, 96:192] = low

    def deriv_operators():
        for d in range(3):
            square[0:64, 0:64] = deriv[d]
            high, low = halves(square[...].T[0:64, 0:64])
            w_slope[d * 64 : (d + 1) * 64, 0:64] = high
            w_slope[d * 64 : (d + 1) * 64, 64:128] = high
            w_slope[d * 64 : (d + 1) * 64, 128:192] = low

    def face_copy(step, at, side, target):
        return pltpu.make_async_remote_copy(
            src_ref=sendb.at[step, at],
            dst_ref=recvb.at[step, side],
            send_sem=face_send.at[max(at - 2, 0)],
            recv_sem=face_recv.at[step, max(side - 2, 0)],
            device_id=target,
            device_id_type=MESH,
        )

    def face_copies(step):
        return (
            face_copy(step, 0, 1, (lax.rem(a + na - 1, na), m, w)),
            face_copy(step, 1, 0, (lax.rem(a + 1, na), m, w)),
            face_copy(step, 2, 2, (a, m, 1 - w)),
            face_copy(step, 3, 4, (a, jnp.maximum(m - 1, 0), w)),
            face_copy(step, 4, 3, (a, jnp.minimum(m + 1, nm - 1), w)),
        )

    def three_faces(step):
        return pltpu.make_async_remote_copy(
            src_ref=sendb.at[step, 0:3],
            dst_ref=recvb.at[step, 0:3],
            send_sem=face_send.at[0],
            recv_sem=face_recv.at[step, 0],
            device_id=(a, m, 1 - w),
            device_id_type=MESH,
        )

    def sent_faces(step):
        three_faces(step).wait_send()
        copies = face_copies(step)
        pl.when(m > 0)(copies[3].wait_send)
        pl.when(m < nm - 1)(copies[4].wait_send)

    def split(v, value):
        high, low = halves(value)
        cat[v, 0:64] = high
        cat[v, 64:128] = low
        cat[v, 128:192] = high

    def first_traces():
        for v in range(NV):
            split(v, adj[v])
            trace[v] = dot(w_trace[...], cat[v])

    def later_traces():
        for v in range(NV):
            added = dot(w_pair[...], jcat[v])
            trace[v] = ahead[v] - 0.25 * (added[0:96] + added[96:192])

    def update(v, target):
        lifted = dot(w_lift[...], jcat[v])
        target[v] = base[v] - 0.25 * (lifted[0:64] + lifted[64:128])

    def bottom_of(ref, v, row):
        rows = slice(row, row + FPTS)
        value = ref[v, rows, 0:TILE]
        for ex in range(1, EX):
            value = jnp.where(
                along == ex, pltpu.roll(ref[v, rows, ex * TILE : (ex + 1) * TILE], ex, 1), value
            )
        return value

    def pack(step):
        for v in range(NV):
            sendb[step, 0, v] = tile_of(trace, v, 0, 0)
            sendb[step, 1, v] = tile_of(trace, v, 1, EX - 1)
        copies = face_copies(step)
        copies[0].start()
        copies[1].start()
        for v in range(NV):
            low_y = tile_of(trace, v, 2, 0)
            for ex in range(1, EX):
                low_y = jnp.where(strip == ex, pltpu.roll(tile_of(trace, v, 2, ex), 32 * ex, 1), low_y)
            sendb[step, 3, v] = low_y
            high_y = tile_of(trace, v, 3, EX - 1)
            for ex in range(EX - 1):
                high_y = jnp.where(
                    strip == ex, pltpu.roll(tile_of(trace, v, 3, ex), 32 * (ex + 1), 1), high_y
                )
            sendb[step, 4, v] = high_y
        pl.when(m > 0)(copies[3].start)
        pl.when(m < nm - 1)(copies[4].start)
        for v in range(NV):
            low_z = tile_of(trace, v, 4, 0)
            high_z = pltpu.roll(tile_of(trace, v, 5, 0), 97, 1)
            for ex in range(1, EX):
                low_z = jnp.where(along == ex, pltpu.roll(tile_of(trace, v, 4, ex), ex, 1), low_z)
                high_z = jnp.where(along == ex, pltpu.roll(tile_of(trace, v, 5, ex), 97 + ex, 1), high_z)
            zown[v] = low_z * WALL_SIGN[v]
            sendb[step, 2, v] = jnp.where(w == 0, high_z, low_z)
        copies[2].start()

    def inner_part(step):
        for v in range(NV):
            if step > 0:
                update(v, adj)
                split(v, adj[v])
            slopes[v] = dot(w_slope[...], cat[v])

        def chunk(i, carry):
            row = pl.multiple_of((i >> 2) * 16, 16)
            rows = pl.ds(row, 16)
            lanes = pl.ds(pl.multiple_of((i & 3) * TILE, TILE), TILE)
            metric = [met[d, rows, lanes].astype(F32) for d in range(3)]
            slope = []
            for x in range(NV):
                total = metric[0] * slopes[x, rows, lanes]
                for d in range(1, 3):
                    total = total + metric[d] * slopes[x, pl.ds(d * 64 + row, 16), lanes]
                slope.append(total)
            for u in range(NV):
                flux = jac[u, rows, lanes].astype(F32) * slope[0]
                for x in range(1, NV):
                    flux = flux + jac[x * NV + u, rows, lanes].astype(F32) * slope[x]
                base[u, rows, lanes] = adj[u, rows, lanes] + 0.25 * (src[u, rows, lanes] - flux)
            return carry

        lax.fori_loop(0, 16, chunk, 0)
        if step < STEPS - 1:
            for v in range(NV):
                split(v, base[v])
                ahead[v] = dot(w_trace[...], cat[v])

        for v in range(NV):
            for ex in range(EX):
                lanes = slice(ex * TILE, (ex + 1) * TILE)
                parts = (
                    tile_of(trace, v, 1, ex - 1) if ex > 0 else None,
                    tile_of(trace, v, 0, ex + 1) if ex < EX - 1 else None,
                    jnp.where(strip == 0, 0.0, pltpu.roll(tile_of(trace, v, 3, ex), 32, 1)),
                    jnp.where(strip == 3, 0.0, pltpu.roll(tile_of(trace, v, 2, ex), 96, 1)),
                    jnp.where(along == 0, 0.0, pltpu.roll(tile_of(trace, v, 5, ex), 1, 1)),
                    jnp.where(along == 31, 0.0, pltpu.roll(tile_of(trace, v, 4, ex), 127, 1)),
                )
                for side, part in enumerate(parts):
                    rows = slice(side * FPTS, (side + 1) * FPTS)
                    own = tile_of(trace, v, side, ex)
                    jump[v, rows, lanes] = pen[rows, lanes] * (own if part is None else own - part)

    def wait_faces(step):
        three_faces(step).wait_recv()
        copies = face_copies(step)
        pl.when(m > 0)(copies[4].wait_recv)
        pl.when(m < nm - 1)(copies[3].wait_recv)

    def align(step):
        for side in range(4):
            faces = jnp.broadcast_to(match[side : side + 1, :], (FPTS, TILE))
            for v in range(NV):
                matched = jnp.take_along_axis(
                    recvb[step, (0, 1, 3, 4)[side], v], faces, axis=1
                )
                for half in (0, 8):
                    index = turn[side, half : half + 8]
                    low = jnp.take_along_axis(matched[0:8], index & 7, axis=0)
                    high = jnp.take_along_axis(matched[8:16], index & 7, axis=0)
                    arrived[side, v, half : half + 8] = jnp.where(index < 8, low, high)

    def outer_part(step):
        for v in range(NV):
            z_low = jnp.where(w == 0, zown[v], recvb[step, 2, v])
            z_high = jnp.where(w == 0, recvb[step, 2, v], 0.0)
            first = slice(0, TILE)
            last = slice(E - TILE, E)
            jump[v, 0:16, first] = jump[v, 0:16, first] - pen[0:16, first] * arrived[0, v]
            jump[v, 16:32, last] = jump[v, 16:32, last] - pen[16:32, last] * arrived[1, v]
            for ex in range(EX):
                lanes = slice(ex * TILE, (ex + 1) * TILE)
                low_y = arrived[2, v]
                high_y = arrived[3, v]
                low_y = low_y if ex == 0 else pltpu.roll(low_y, TILE - 32 * ex, 1)
                high_y = high_y if ex == EX - 1 else pltpu.roll(high_y, 96 - 32 * ex, 1)
                low_z = z_low if ex == 0 else pltpu.roll(z_low, TILE - ex, 1)
                high_z = pltpu.roll(z_high, 31 - ex, 1)
                edges = (
                    jnp.where(strip == 0, low_y, 0.0),
                    jnp.where(strip == 3, high_y, 0.0),
                    jnp.where(along == 0, low_z, 0.0),
                    jnp.where(along == 31, high_z, 0.0),
                )
                for side, edge in enumerate(edges, start=2):
                    rows = slice(side * FPTS, (side + 1) * FPTS)
                    jump[v, rows, lanes] = jump[v, rows, lanes] - pen[rows, lanes] * edge
            high, low = halves(jump[v])
            jcat[v, 0:96] = high
            jcat[v, 96:192] = low

    def plan_routes():
        for side in range(4):
            turn[side] = turned_points(orient[side : side + 1, :])
        count = owner.shape[1]
        block = cells[...] >> 8
        at_block = (iota((count, PTS), 0) == block).astype(F32).astype(BF16)
        owners = jnp.broadcast_to(owner[...].astype(F32), (8, count)).astype(BF16)
        target = dot(owners, at_block)[0:1].astype(I32)
        earlier = (iota((PTS, PTS), 0) < iota((PTS, PTS), 1)).astype(F32).astype(BF16)
        before = dot(at_block, earlier)
        slot = jnp.sum(at_block.astype(F32) * before, axis=0, keepdims=True).astype(I32)
        hit = (iota((count, PTS), 0) == target).astype(F32).astype(BF16)
        to_owner[:, 0:PTS] = hit
        to_owner[:, PTS : 2 * PTS] = hit
        slot_mask[...] = ((iota((8, PTS), 0) & 1) == slot).astype(F32)
        message[...] = jnp.zeros((TILE, 2 * PTS), BF16)
        offs[...] = (cells[...] & (BLOCK - 1)).astype(F32)
        point = iota((1, PTS), 1) >> 4
        spot = jnp.zeros((1, PTS), I32)
        for n in range(PTS // FPTS):
            face = wall_list[n]
            spot = jnp.where(point == n, (face & 3) * 32 + (face >> 2), spot)
        pick = (iota((TILE, PTS), 0) == spot).astype(F32).astype(BF16)
        spread[0:TILE] = pick
        spread[TILE : 2 * TILE] = pick

    def at_z_low(values):
        added = dot(jnp.concatenate([w_pair[64:80], w_pair[160:176]], axis=0), values)
        return 0.25 * (added[0:16] + added[16:32])

    def bottom_ahead():
        for side in range(5):
            rows = slice(side * FPTS, (side + 1) * FPTS)
            value = pen[rows, 0:TILE]
            for ex in range(1, EX):
                value = jnp.where(
                    along == ex, pltpu.roll(pen[rows, ex * TILE : (ex + 1) * TILE], ex, 1), value
                )
            pen_low[rows] = value
        for v in range(NV):
            lanes = slice(v * TILE, (v + 1) * TILE)
            for part in range(4):
                rows = slice(part * FPTS, (part + 1) * FPTS)
                high, low = halves(bottom_of(base, v, part * FPTS))
                packed[rows, lanes] = high
                packed[64 + part * FPTS : 80 + part * FPTS, lanes] = low
                packed[128 + part * FPTS : 144 + part * FPTS, lanes] = high
        wall_ahead[...] = dot(w_trace[64:80], packed[...])
        for v in range(NV):
            lanes = slice(v * TILE, (v + 1) * TILE)
            for side in range(6):
                high, low = halves(bottom_of(jump, v, side * FPTS))
                packed[side * FPTS : (side + 1) * FPTS, lanes] = high
                packed[96 + side * FPTS : 112 + side * FPTS, lanes] = low
        wall_ahead[...] = wall_ahead[...] - at_z_low(packed[...])
        packed[80:96] = jnp.zeros((FPTS, NV * TILE), BF16)
        packed[176:192] = jnp.zeros((FPTS, NV * TILE), BF16)

    def wall_points():
        for v in range(NV):
            lanes = slice(v * TILE, (v + 1) * TILE)
            low_y = jnp.zeros((FPTS, TILE), F32)
            high_y = jnp.zeros((FPTS, TILE), F32)
            for ex in range(EX):
                from_low = arrived[2, v] if ex == 0 else pltpu.roll(arrived[2, v], TILE - 31 * ex, 1)
                low_y = jnp.where(lane == ex, from_low, low_y)
                from_high = pltpu.roll(arrived[3, v], 96 - 31 * ex, 1)
                high_y = jnp.where(lane == 96 + ex, from_high, high_y)
            edges = (
                jnp.where(along == 0, arrived[0, v], 0.0),
                jnp.where(along == EX - 1, pltpu.roll(arrived[1, v], EX - 1, 1), 0.0),
                low_y,
                high_y,
                zown[v],
            )
            for side, edge in enumerate(edges):
                rows = slice(side * FPTS, (side + 1) * FPTS)
                high, low = halves(pen_low[rows] * edge)
                packed[rows, lanes] = high
                packed[96 + side * FPTS : 112 + side * FPTS, lanes] = low
        at_wall = wall_ahead[...] + at_z_low(packed[...])
        rows = jnp.concatenate([at_wall[:, v * TILE : (v + 1) * TILE] for v in range(NV)], axis=0)
        high, low = halves(rows)
        expanded = dot(jnp.concatenate([high, low], axis=1), spread[...])
        own_point = (iota((FPTS, PTS), 1) & 15) == iota((FPTS, PTS), 0)
        sens = [jnp.zeros((1, PTS), F32) for c in range(3)]
        for v in range(NV):
            values = jnp.where(own_point, expanded[v * FPTS : (v + 1) * FPTS], 0.0)
            line = jnp.sum(values, axis=0, keepdims=True)
            for c in range(3):
                sens[c] = sens[c] + geom[v, c : c + 1, :].astype(F32) * line
        field = iota((8, PTS), 0) >> 1
        values = jnp.broadcast_to(offs[...], (8, PTS))
        for c in range(3):
            values = jnp.where(field == c, sens[c], values)
        high, low = halves(values * slot_mask[...])
        blank = jnp.zeros((8, PTS), BF16)
        message[0:16, 0:PTS] = jnp.concatenate([high, blank], axis=0)
        message[0:16, PTS : 2 * PTS] = jnp.concatenate([low, blank], axis=0)
        goes[...] = dot_nt(to_owner[...], message[...])

    mine = a * nm + m
    owners = na * group

    def owner_copy(offset, j):
        to, place = lax.rem(a + offset, na), lax.rem(here + j, group)
        return pltpu.make_async_remote_copy(
            src_ref=goes.at[pl.ds(to * group + place, 1)],
            dst_ref=came.at[pl.ds(mine, 1)],
            send_sem=hop_sem.at[0],
            recv_sem=hop_sem.at[1],
            device_id=(to, place // nw, lax.rem(place, nw)),
            device_id_type=MESH,
        )

    def owner_bytes(ref, count):
        return pltpu.make_async_remote_copy(
            src_ref=ref.at[0:count],
            dst_ref=ref.at[0:count],
            send_sem=hop_sem.at[0],
            recv_sem=hop_sem.at[1],
            device_id=(a, m, 1 - w),
            device_id_type=MESH,
        )

    def tell_line():
        for j in range(1, group):
            other = lax.rem(here + j, group)
            pl.semaphore_signal(
                told.at[2],
                inc=1,
                device_id=(a, other // nw, lax.rem(other, nw)),
                device_id_type=MESH,
            )

    loaded(0)
    interp_operators()
    loaded(1)
    first_traces()
    pl.semaphore_wait(barrier, len(near) + group - 1)
    pack(0)
    tell(0, second)
    loaded(2)
    pair_operators()
    deriv_operators()
    plan_routes()
    loaded(3)
    pen[...] = pen16[...].astype(F32)
    inner_part(0)
    hear(0, second)
    tell(1, third)
    wait_faces(0)
    align(0)
    outer_part(0)
    later_traces()
    sent_faces(0)
    pack(1)
    inner_part(1)

    @pl.when(w == 0)
    def _():
        bottom_ahead()

    hear(1, third)
    tell_line()
    wait_faces(1)
    align(1)

    @pl.when(w == 0)
    def _():
        wall_points()

    pl.semaphore_wait(told.at[2], group - 1)

    @pl.when(w == 0)
    def _():
        for offset in far_first(na):
            for j in range(group):
                if offset or j:
                    owner_copy(offset, j).start()
        came[pl.ds(mine, 1)] = goes[pl.ds(a * group + here, 1)]

    outer_part(1)
    for v in range(NV):
        update(v, out)

    @pl.when(w == 0)
    def _():
        owner_bytes(came, na * nm - 1).wait_recv()

    @pl.when(w != 0)
    def _():
        owner_bytes(came, na * nm).wait_recv()

    rows = came[...]
    column = iota((na * nm, BLOCK), 1).astype(F32)
    sums = [jnp.zeros((na * nm, BLOCK), F32) for c in range(3)]
    for slot in range(2):
        hit = rows[:, 6 + slot : 7 + slot] == column
        for c in range(3):
            at = 2 * c + slot
            sums[c] = sums[c] + jnp.where(hit, rows[:, at : at + 1], 0.0)
    for c in range(3):
        ffd[c : c + 1, :] = jnp.sum(sums[c], axis=0, keepdims=True)

    sent_faces(STEPS - 1)

    @pl.when(w == 0)
    def _():
        owner_bytes(goes, owners - 1).wait_send()


def solution(mesh):
    sizes = tuple(mesh.shape[name] for name in ("azim", "merid", "wall"))
    na, nm, nw = sizes
    group = nm * nw
    faces = (STEPS, 5, NV, FPTS, TILE)
    scratch = [
        pltpu.VMEM((NV, NSP, E), F32),
        pltpu.VMEM((NV, NSP, E), F32),
        pltpu.VMEM((NV * NV, NSP, E), BF16),
        pltpu.VMEM((3, NSP, E), BF16),
        pltpu.VMEM((NFP, E), BF16),
        pltpu.VMEM((3, NSP, NSP), F32),
        pltpu.VMEM((NSP, NFP), F32),
        pltpu.VMEM((4, TILE), I32),
        pltpu.VMEM((4, TILE), I32),
        pltpu.SMEM((PTS // FPTS,), I32),
        pltpu.VMEM((NV, 3, PTS), BF16),
        pltpu.VMEM((1, PTS), I32),
        pltpu.VMEM((1, na * group), I32),
        pltpu.VMEM((NFP, E), F32),
        pltpu.VMEM((NV, NFP, E), F32),
        pltpu.VMEM((NV, 3 * NSP, E), F32),
        pltpu.VMEM((NV, 3 * NSP, E), BF16),
        pltpu.VMEM((NV, NSP, E), F32),
        pltpu.VMEM((NV, NFP, E), F32),
        pltpu.VMEM((NV, 2 * NFP, E), BF16),
        pltpu.VMEM((NFP, 3 * NSP), BF16),
        pltpu.VMEM((3 * NSP, 3 * NSP), BF16),
        pltpu.VMEM((2 * NSP, 2 * NFP), BF16),
        pltpu.VMEM((2 * NFP, 2 * NFP), BF16),
        pltpu.VMEM((NV, NFP, E), F32),
        pltpu.VMEM((4, NV, FPTS, TILE), F32),
        pltpu.VMEM((5 * FPTS, TILE), F32),
        pltpu.VMEM((FPTS, NV * TILE), F32),
        pltpu.VMEM((TILE, TILE), F32),
        pltpu.VMEM((4, FPTS, TILE), I32),
        pltpu.VMEM(faces, F32),
        pltpu.VMEM(faces, F32),
        pltpu.VMEM((NV, FPTS, TILE), F32),
        pltpu.VMEM((3 * NSP, NV * TILE), BF16),
        pltpu.VMEM((8, PTS), F32),
        pltpu.VMEM((na * group, 2 * PTS), BF16),
        pltpu.VMEM((2 * TILE, PTS), BF16),
        pltpu.VMEM((1, PTS), F32),
        pltpu.VMEM((TILE, 2 * PTS), BF16),
        pltpu.VMEM((na * group, TILE), F32),
        pltpu.VMEM((na * nm, TILE), F32),
        pltpu.SemaphoreType.DMA((4,)),
        pltpu.SemaphoreType.DMA((3,)),
        pltpu.SemaphoreType.DMA((STEPS, 3)),
        pltpu.SemaphoreType.DMA((2,)),
        pltpu.SemaphoreType.REGULAR((3,)),
    ]
    hbm = pl.BlockSpec(memory_space=pltpu.HBM)
    vmem = pl.BlockSpec(memory_space=pltpu.VMEM)
    call = pl.pallas_call(
        functools.partial(kernel, sizes),
        out_shape=(pltpu.VMEM((NV, NSP, E), F32), pltpu.VMEM((3, BLOCK), F32)),
        in_specs=[hbm] * 13,
        out_specs=(vmem, vmem),
        scratch_shapes=scratch,
        compiler_params=pltpu.CompilerParams(
            collective_id=0, has_side_effects=True, vmem_limit_bytes=40 * 1024 * 1024
        ),
        name="adjoint_steps",
    )

    def per_device(
        adjoint_in,
        source,
        jacobian,
        metric,
        penalty,
        deriv,
        interp,
        face_match,
        orientation,
        wall_faces,
        wall_geometry,
        lattice_cells,
        block_owner,
    ):
        operands = (
            adjoint_in.reshape(NV, NSP, E),
            source.reshape(NV, NSP, E),
            jacobian.reshape(NV * NV, NSP, E),
            metric.reshape(3, NSP, E),
            penalty.reshape(NFP, E),
            deriv,
            interp.T,
            face_match.reshape(4, TILE),
            orientation.reshape(4, TILE),
            wall_faces.reshape(-1),
            wall_geometry.reshape(3, NV, PTS).transpose(1, 0, 2),
            lattice_cells.reshape(1, PTS),
            block_owner.reshape(1, -1),
        )
        adjoint, owned = call(
            *(pltpu.with_memory_space_constraint(operand, pltpu.HBM) for operand in operands)
        )
        return adjoint[None, None, None], owned

    placed = (
        P("azim", "merid", "wall", None, None, None),
        P("azim", "merid", "wall", None, None, None),
        P("azim", "merid", "wall", None, None, None, None),
        P("azim", "merid", "wall", None, None, None),
        P("azim", "merid", "wall", None, None),
        P(),
        P(),
        P("azim", "merid", "wall", None, None),
        P("azim", "merid", "wall", None, None),
        P("azim", "merid", None),
        P("azim", "merid", None, None, None),
        P("azim", "merid", None),
        P(),
    )
    return jax.shard_map(
        per_device,
        mesh=mesh,
        in_specs=placed,
        out_specs=(
            P("azim", "merid", "wall", None, None, None),
            P(None, ("azim", "merid", "wall")),
        ),
        check_vma=False,
    )
```

```python
import functools

import jax
import jax.numpy as jnp
from jax import lax
from jax.experimental import pallas as pl
from jax.experimental.pallas import tpu as pltpu
from jax.sharding import PartitionSpec as P

MESH = pl.DeviceIdType.MESH
F32, BF16, I32 = jnp.float32, jnp.bfloat16, jnp.int32

NV = 5
NSP = 64
FPTS = 16
NFP = 96
EX = 4
E = 512
PTS = 256
STEPS = 2
BLOCK = 256
TILE = 128
PARTS = (slice(0, 3), slice(3, 5))
WALL_SIGN = (1.0, 1.0, 1.0, -1.0, 1.0)


def iota(shape, axis):
    return lax.broadcasted_iota(I32, shape, axis)


def halves(value):
    high = value.astype(BF16)
    low = (value - high.astype(F32)).astype(BF16)
    return high, low


def dot(left, right):
    return jnp.dot(left, right, preferred_element_type=F32)


def dot_nt(left, right):
    return lax.dot_general(left, right, (((1,), (1,)), ((), ())), preferred_element_type=F32)


def rounds(count):
    def offsets(steps):
        return tuple(sorted({step % count for step in steps} - {0}))

    near, second, third = offsets((1, -1, 2, -2, 8, -8)), offsets((2, -2, 8, -8)), offsets((4, -4, 16))
    one = {0, *near}
    two = one | {(i + j) % count for i in one for j in second}
    all_known = two | {(i + j) % count for i in two for j in third}
    if len(all_known) == count and set(second) <= one and set(third) <= two:
        return near, second, third
    return offsets(range(count)), (), ()


def far_first(count):
    def hops(offset):
        y, z = divmod(offset, 8)
        return min(y, 4 - y) + min(z, 8 - z)

    return sorted(range(count), key=hops, reverse=True)


def turned_points(code):
    row = iota((FPTS, TILE), 0)
    i, k = row >> 2, row & 3
    first = jnp.where((code & 4) != 0, k, i)
    second = jnp.where((code & 4) != 0, i, k)
    first = jnp.where((code & 1) != 0, 3 - first, first)
    second = jnp.where((code & 2) != 0, 3 - second, second)
    return first * 4 + second


def tile_of(ref, v, side, ex):
    return ref[v, side * FPTS : (side + 1) * FPTS, ex * TILE : (ex + 1) * TILE]


def kernel(
    sizes,
    adj_hbm,
    src_hbm,
    jac_hbm,
    met_hbm,
    pen_hbm,
    deriv_hbm,
    interp_hbm,
    match_hbm,
    orient_hbm,
    list_hbm,
    geom_hbm,
    cells_hbm,
    owner_hbm,
    out,
    ffd,
    adj,
    src,
    jac,
    met,
    pen16,
    deriv,
    interp_t,
    match,
    orient,
    wall_list,
    geom,
    cells,
    owner,
    pen,
    trace,
    slopes,
    cat,
    base,
    jump,
    jcat,
    w_trace,
    w_slope,
    w_lift,
    w_pair,
    ahead,
    arrived,
    pen_low,
    wall_ahead,
    square,
    turn,
    sendb,
    recvb,
    zown,
    packed,
    slot_mask,
    to_owner,
    spots,
    offs,
    message,
    goes,
    came,
    load_sem,
    face_send,
    face_recv,
    hop_sem,
    told,
):
    na, nm, nw = sizes
    group = nm * nw
    a, m, w = lax.axis_index("azim"), lax.axis_index("merid"), lax.axis_index("wall")
    here = m * nw + w

    groups = (
        ((interp_hbm, interp_t),),
        ((adj_hbm, adj),),
        (
            (deriv_hbm, deriv),
            (match_hbm, match),
            (cells_hbm, cells),
            (owner_hbm, owner),
            (list_hbm, wall_list),
            (orient_hbm, orient),
        ),
        (
            (pen_hbm, pen16),
            (met_hbm, met),
            (jac_hbm, jac),
            (src_hbm, src),
            (geom_hbm, geom),
        ),
    )
    loads = [
        [pltpu.make_async_copy(*pair, load_sem.at[i]) for pair in group_here]
        for i, group_here in enumerate(groups)
    ]
    for part in loads[:2]:
        for load in part:
            load.start()

    def loaded(part):
        for load in loads[part]:
            load.wait()

    near, second, third = rounds(na)
    barrier = pltpu.get_barrier_semaphore()

    def sector(offset):
        return lax.rem(a + offset, na), m, w

    for offset in far_first(na):
        if offset in near:
            pl.semaphore_signal(barrier, inc=1, device_id=sector(offset), device_id_type=MESH)
    for j in sorted(range(1, group), key=lambda step: abs(step - group // 2)):
        other = lax.rem(here + j, group)
        pl.semaphore_signal(
            barrier, inc=1, device_id=(a, other // nw, lax.rem(other, nw)), device_id_type=MESH
        )
    for part in loads[2:]:
        for load in part:
            load.start()

    def tell(at, offsets):
        for offset in offsets:
            pl.semaphore_signal(
                told.at[at], inc=1, device_id=sector(offset), device_id_type=MESH
            )

    def hear(at, offsets):
        if offsets:
            pl.semaphore_wait(told.at[at], len(offsets))

    lane = iota((FPTS, TILE), 1)
    strip = lane >> 5
    along = lane & 31

    def interp_operators():
        square[0:64, 0:96] = interp_t[...]
        high, low = halves(square[...].T[0:96, 0:64])
        w_trace[:, 0:64] = high
        w_trace[:, 64:128] = high
        w_trace[:, 128:192] = low
        high, low = halves(interp_t[...])
        w_lift[0:64, 0:96] = high
        w_lift[0:64, 96:192] = high
        w_lift[64:128, 0:96] = low
        w_lift[64:128, 96:192] = low

    def pair_operators():
        pair = dot(w_trace[...], jnp.concatenate([*halves(interp_t[...]), halves(interp_t[...])[0]], axis=0))
        high, low = halves(pair)
        w_pair[0:96, 0:96] = high
        w_pair[0:96, 96:192] = high
        w_pair[96:192, 0:96] = low
        w_pair[96:192, 96:192] = low

    def deriv_operators():
        for d in range(3):
            square[0:64, 0:64] = deriv[d]
            high, low = halves(square[...].T[0:64, 0:64])
            w_slope[d * 64 : (d + 1) * 64, 0:64] = high
            w_slope[d * 64 : (d + 1) * 64, 64:128] = high
            w_slope[d * 64 : (d + 1) * 64, 128:192] = low

    def face_copy(step, at, side, target, part=slice(0, NV)):
        return pltpu.make_async_remote_copy(
            src_ref=sendb.at[step, at, part],
            dst_ref=recvb.at[step, side, part],
            send_sem=face_send.at[max(at - 2, 0)],
            recv_sem=face_recv.at[step, max(side - 2, 0)],
            device_id=target,
            device_id_type=MESH,
        )

    def x_copies(step, part):
        return (
            face_copy(step, 0, 1, sector(na - 1), part),
            face_copy(step, 1, 0, sector(1), part),
            face_copy(step, 2, 2, (a, m, 1 - w), part),
        )

    def y_low_copy(step, part=slice(0, NV)):
        return face_copy(step, 3, 4, (a, jnp.maximum(m - 1, 0), w), part)

    def y_high_copy(step, part=slice(0, NV)):
        return face_copy(step, 4, 3, (a, jnp.minimum(m + 1, nm - 1), w), part)

    def three_faces(step):
        return pltpu.make_async_remote_copy(
            src_ref=sendb.at[step, 0:3],
            dst_ref=recvb.at[step, 0:3],
            send_sem=face_send.at[0],
            recv_sem=face_recv.at[step, 0],
            device_id=(a, m, 1 - w),
            device_id_type=MESH,
        )

    def sent_faces(step):
        three_faces(step).wait_send()
        pl.when(m > 0)(y_low_copy(step).wait_send)
        pl.when(m < nm - 1)(y_high_copy(step).wait_send)

    def split(v, value):
        high, low = halves(value)
        cat[v, 0:64] = high
        cat[v, 64:128] = low
        cat[v, 128:192] = high

    def first_trace(v):
        split(v, adj[v])
        trace[v] = dot(w_trace[...], cat[v])

    def later_trace(v):
        added = dot(w_pair[...], jcat[v])
        trace[v] = ahead[v] - 0.25 * (added[0:96] + added[96:192])

    def update(v, target):
        lifted = dot(w_lift[...], jcat[v])
        target[v] = base[v] - 0.25 * (lifted[0:64] + lifted[64:128])

    def bottom_of(ref, v, row):
        rows = slice(row, row + FPTS)
        value = ref[v, rows, 0:TILE]
        for ex in range(1, EX):
            value = jnp.where(
                along == ex, pltpu.roll(ref[v, rows, ex * TILE : (ex + 1) * TILE], ex, 1), value
            )
        return value

    def pack(step, v):
        low_y = tile_of(trace, v, 2, 0)
        for ex in range(1, EX):
            low_y = jnp.where(strip == ex, pltpu.roll(tile_of(trace, v, 2, ex), 32 * ex, 1), low_y)
        sendb[step, 3, v] = low_y
        high_y = tile_of(trace, v, 3, EX - 1)
        for ex in range(EX - 1):
            high_y = jnp.where(
                strip == ex, pltpu.roll(tile_of(trace, v, 3, ex), 32 * (ex + 1), 1), high_y
            )
        sendb[step, 4, v] = high_y
        sendb[step, 0, v] = tile_of(trace, v, 0, 0)
        sendb[step, 1, v] = tile_of(trace, v, 1, EX - 1)
        low_z = tile_of(trace, v, 4, 0)
        high_z = pltpu.roll(tile_of(trace, v, 5, 0), 97, 1)
        for ex in range(1, EX):
            low_z = jnp.where(along == ex, pltpu.roll(tile_of(trace, v, 4, ex), ex, 1), low_z)
            high_z = jnp.where(along == ex, pltpu.roll(tile_of(trace, v, 5, ex), 97 + ex, 1), high_z)
        zown[v] = low_z * WALL_SIGN[v]
        sendb[step, 2, v] = jnp.where(w == 0, high_z, low_z)

    def send_faces(step, part):
        pl.when(m > 0)(y_low_copy(step, part).start)
        pl.when(m < nm - 1)(y_high_copy(step, part).start)
        for copy in x_copies(step, part):
            copy.start()

    def inner_part(step):
        for v in range(NV):
            if step > 0:
                update(v, adj)
                split(v, adj[v])
            slopes[v] = dot(w_slope[...], cat[v])

        def chunk(i, carry):
            row = pl.multiple_of((i >> 2) * 16, 16)
            rows = pl.ds(row, 16)
            lanes = pl.ds(pl.multiple_of((i & 3) * TILE, TILE), TILE)
            metric = [met[d, rows, lanes].astype(F32) for d in range(3)]
            slope = []
            for x in range(NV):
                total = metric[0] * slopes[x, rows, lanes]
                for d in range(1, 3):
                    total = total + metric[d] * slopes[x, pl.ds(d * 64 + row, 16), lanes]
                slope.append(total)
            for u in range(NV):
                flux = jac[u, rows, lanes].astype(F32) * slope[0]
                for x in range(1, NV):
                    flux = flux + jac[x * NV + u, rows, lanes].astype(F32) * slope[x]
                base[u, rows, lanes] = adj[u, rows, lanes] + 0.25 * (src[u, rows, lanes] - flux)
            return carry

        lax.fori_loop(0, 16, chunk, 0)
        if step < STEPS - 1:
            for v in range(NV):
                split(v, base[v])
                ahead[v] = dot(w_trace[...], cat[v])

        for v in range(NV):
            for ex in range(EX):
                lanes = slice(ex * TILE, (ex + 1) * TILE)
                parts = (
                    tile_of(trace, v, 1, ex - 1) if ex > 0 else None,
                    tile_of(trace, v, 0, ex + 1) if ex < EX - 1 else None,
                    jnp.where(strip == 0, 0.0, pltpu.roll(tile_of(trace, v, 3, ex), 32, 1)),
                    jnp.where(strip == 3, 0.0, pltpu.roll(tile_of(trace, v, 2, ex), 96, 1)),
                    jnp.where(along == 0, 0.0, pltpu.roll(tile_of(trace, v, 5, ex), 1, 1)),
                    jnp.where(along == 31, 0.0, pltpu.roll(tile_of(trace, v, 4, ex), 127, 1)),
                )
                for side, part in enumerate(parts):
                    rows = slice(side * FPTS, (side + 1) * FPTS)
                    own = tile_of(trace, v, side, ex)
                    jump[v, rows, lanes] = pen[rows, lanes] * (own if part is None else own - part)

    def wait_faces(step):
        three_faces(step).wait_recv()
        pl.when(m > 0)(y_high_copy(step).wait_recv)
        pl.when(m < nm - 1)(y_low_copy(step).wait_recv)

    def align(step):
        for side in range(4):
            faces = jnp.broadcast_to(match[side : side + 1, :], (FPTS, TILE))
            for v in range(NV):
                matched = jnp.take_along_axis(
                    recvb[step, (0, 1, 3, 4)[side], v], faces, axis=1
                )
                for half in (0, 8):
                    index = turn[side, half : half + 8]
                    low = jnp.take_along_axis(matched[0:8], index & 7, axis=0)
                    high = jnp.take_along_axis(matched[8:16], index & 7, axis=0)
                    arrived[side, v, half : half + 8] = jnp.where(index < 8, low, high)

    def outer_part(step):
        for v in range(NV):
            z_low = jnp.where(w == 0, zown[v], recvb[step, 2, v])
            z_high = jnp.where(w == 0, recvb[step, 2, v], 0.0)
            first = slice(0, TILE)
            last = slice(E - TILE, E)
            jump[v, 0:16, first] = jump[v, 0:16, first] - pen[0:16, first] * arrived[0, v]
            jump[v, 16:32, last] = jump[v, 16:32, last] - pen[16:32, last] * arrived[1, v]
            for ex in range(EX):
                lanes = slice(ex * TILE, (ex + 1) * TILE)
                low_y = arrived[2, v]
                high_y = arrived[3, v]
                low_y = low_y if ex == 0 else pltpu.roll(low_y, TILE - 32 * ex, 1)
                high_y = high_y if ex == EX - 1 else pltpu.roll(high_y, 96 - 32 * ex, 1)
                low_z = z_low if ex == 0 else pltpu.roll(z_low, TILE - ex, 1)
                high_z = pltpu.roll(z_high, 31 - ex, 1)
                edges = (
                    jnp.where(strip == 0, low_y, 0.0),
                    jnp.where(strip == 3, high_y, 0.0),
                    jnp.where(along == 0, low_z, 0.0),
                    jnp.where(along == 31, high_z, 0.0),
                )
                for side, edge in enumerate(edges, start=2):
                    rows = slice(side * FPTS, (side + 1) * FPTS)
                    jump[v, rows, lanes] = jump[v, rows, lanes] - pen[rows, lanes] * edge
            high, low = halves(jump[v])
            jcat[v, 0:96] = high
            jcat[v, 96:192] = low

    def plan_routes():
        for side in range(4):
            turn[side] = turned_points(orient[side : side + 1, :])
        count = owner.shape[1]
        block = cells[...] >> 8
        at_block = (iota((count, PTS), 0) == block).astype(F32).astype(BF16)
        owners = jnp.broadcast_to(owner[...].astype(F32), (8, count)).astype(BF16)
        target = dot(owners, at_block)[0:1].astype(I32)
        earlier = (iota((PTS, PTS), 0) < iota((PTS, PTS), 1)).astype(F32).astype(BF16)
        before = dot(at_block, earlier)
        slot = jnp.sum(at_block.astype(F32) * before, axis=0, keepdims=True).astype(I32)
        hit = (iota((count, PTS), 0) == target).astype(F32).astype(BF16)
        to_owner[:, 0:PTS] = hit
        to_owner[:, PTS : 2 * PTS] = hit
        slot_mask[...] = ((iota((8, PTS), 0) & 1) == slot).astype(F32)
        message[...] = jnp.zeros((TILE, 2 * PTS), BF16)
        offs[...] = (cells[...] & (BLOCK - 1)).astype(F32)
        point = iota((1, PTS), 1) >> 4
        spot = jnp.zeros((1, PTS), I32)
        for n in range(PTS // FPTS):
            face = wall_list[n]
            spot = jnp.where(point == n, (face & 3) * 32 + (face >> 2), spot)
        spots[...] = spot

    def at_z_low(values):
        added = dot(jnp.concatenate([w_pair[64:80], w_pair[160:176]], axis=0), values)
        return 0.25 * (added[0:16] + added[16:32])

    def bottom_ahead():
        for side in range(5):
            rows = slice(side * FPTS, (side + 1) * FPTS)
            value = pen[rows, 0:TILE]
            for ex in range(1, EX):
                value = jnp.where(
                    along == ex, pltpu.roll(pen[rows, ex * TILE : (ex + 1) * TILE], ex, 1), value
                )
            pen_low[rows] = value
        for v in range(NV):
            lanes = slice(v * TILE, (v + 1) * TILE)
            for part in range(4):
                rows = slice(part * FPTS, (part + 1) * FPTS)
                high, low = halves(bottom_of(base, v, part * FPTS))
                packed[rows, lanes] = high
                packed[64 + part * FPTS : 80 + part * FPTS, lanes] = low
                packed[128 + part * FPTS : 144 + part * FPTS, lanes] = high
        wall_ahead[...] = dot(w_trace[64:80], packed[...])
        for v in range(NV):
            lanes = slice(v * TILE, (v + 1) * TILE)
            for side in range(6):
                high, low = halves(bottom_of(jump, v, side * FPTS))
                packed[side * FPTS : (side + 1) * FPTS, lanes] = high
                packed[96 + side * FPTS : 112 + side * FPTS, lanes] = low
        wall_ahead[...] = wall_ahead[...] - at_z_low(packed[...])
        packed[80:96] = jnp.zeros((FPTS, NV * TILE), BF16)
        packed[176:192] = jnp.zeros((FPTS, NV * TILE), BF16)

    def wall_points():
        for v in range(NV):
            lanes = slice(v * TILE, (v + 1) * TILE)
            low_y = jnp.take_along_axis(arrived[2, v], (lane & 3) * 32, axis=1)
            high_y = jnp.take_along_axis(arrived[3, v], (lane & 3) * 32, axis=1)
            edges = (
                jnp.where(along == 0, arrived[0, v], 0.0),
                jnp.where(along == EX - 1, pltpu.roll(arrived[1, v], EX - 1, 1), 0.0),
                jnp.where(lane < EX, low_y, 0.0),
                jnp.where((strip == 3) & (along < EX), high_y, 0.0),
                zown[v],
            )
            for side, edge in enumerate(edges):
                rows = slice(side * FPTS, (side + 1) * FPTS)
                high, low = halves(pen_low[rows] * edge)
                packed[rows, lanes] = high
                packed[96 + side * FPTS : 112 + side * FPTS, lanes] = low
        at_wall = wall_ahead[...] + at_z_low(packed[...])
        rows = jnp.concatenate([at_wall[:, v * TILE : (v + 1) * TILE] for v in range(NV)], axis=0)
        expanded = jnp.concatenate(
            [
                jnp.take_along_axis(
                    rows, jnp.broadcast_to(spots[:, i : i + TILE], rows.shape), axis=1
                )
                for i in (0, TILE)
            ],
            axis=1,
        )
        own_point = (iota((FPTS, PTS), 1) & 15) == iota((FPTS, PTS), 0)
        sens = [jnp.zeros((1, PTS), F32) for c in range(3)]
        for v in range(NV):
            values = jnp.where(own_point, expanded[v * FPTS : (v + 1) * FPTS], 0.0)
            line = jnp.sum(values, axis=0, keepdims=True)
            for c in range(3):
                sens[c] = sens[c] + geom[v, c : c + 1, :].astype(F32) * line
        field = iota((8, PTS), 0) >> 1
        values = jnp.broadcast_to(offs[...], (8, PTS))
        for c in range(3):
            values = jnp.where(field == c, sens[c], values)
        high, low = halves(values * slot_mask[...])
        blank = jnp.zeros((8, PTS), BF16)
        message[0:16, 0:PTS] = jnp.concatenate([high, blank], axis=0)
        message[0:16, PTS : 2 * PTS] = jnp.concatenate([low, blank], axis=0)
        goes[...] = dot_nt(to_owner[...], message[...])

    mine = a * nm + m
    owners = na * group

    def owner_copy(offset, j):
        to, place = lax.rem(a + offset, na), lax.rem(here + j, group)
        return pltpu.make_async_remote_copy(
            src_ref=goes.at[pl.ds(to * group + place, 1)],
            dst_ref=came.at[pl.ds(mine, 1)],
            send_sem=hop_sem.at[0],
            recv_sem=hop_sem.at[1],
            device_id=(to, place // nw, lax.rem(place, nw)),
            device_id_type=MESH,
        )

    def owner_bytes(ref, count):
        return pltpu.make_async_remote_copy(
            src_ref=ref.at[0:count],
            dst_ref=ref.at[0:count],
            send_sem=hop_sem.at[0],
            recv_sem=hop_sem.at[1],
            device_id=(a, m, 1 - w),
            device_id_type=MESH,
        )

    def tell_line():
        for j in range(1, group):
            other = lax.rem(here + j, group)
            pl.semaphore_signal(
                told.at[2],
                inc=1,
                device_id=(a, other // nw, lax.rem(other, nw)),
                device_id_type=MESH,
            )

    loaded(0)
    interp_operators()
    loaded(1)
    for part in PARTS:
        for v in range(NV)[part]:
            first_trace(v)
            pack(0, v)
        if part.start == 0:
            pl.semaphore_wait(barrier, len(near) + group - 1)
        send_faces(0, part)
    tell(0, second)

    for end, side in ((0, 3), (nm - 1, 4)):

        @pl.when(m == end)
        def _():
            for step in range(STEPS):
                recvb[step, side] = jnp.zeros((NV, FPTS, TILE), F32)

    loaded(2)
    pair_operators()
    deriv_operators()
    plan_routes()
    loaded(3)
    pen[...] = pen16[...].astype(F32)
    inner_part(0)
    hear(0, second)
    tell(1, third)
    wait_faces(0)
    align(0)
    outer_part(0)
    sent_faces(0)
    for part in PARTS:
        for v in range(NV)[part]:
            later_trace(v)
            pack(1, v)
        send_faces(1, part)
    inner_part(1)

    @pl.when(w == 0)
    def _():
        bottom_ahead()

    hear(1, third)
    tell_line()
    wait_faces(1)
    align(1)

    @pl.when(w == 0)
    def _():
        wall_points()

    pl.semaphore_wait(told.at[2], group - 1)

    @pl.when(w == 0)
    def _():
        for offset in far_first(na):
            for j in range(group):
                if offset or j:
                    owner_copy(offset, j).start()
        came[pl.ds(mine, 1)] = goes[pl.ds(a * group + here, 1)]

    outer_part(1)
    for v in range(NV):
        update(v, out)

    @pl.when(w == 0)
    def _():
        owner_bytes(came, na * nm - 1).wait_recv()

    @pl.when(w != 0)
    def _():
        owner_bytes(came, na * nm).wait_recv()

    rows = came[...]
    column = iota((na * nm, BLOCK), 1).astype(F32)
    sums = [jnp.zeros((na * nm, BLOCK), F32) for c in range(3)]
    for slot in range(2):
        hit = rows[:, 6 + slot : 7 + slot] == column
        for c in range(3):
            at = 2 * c + slot
            sums[c] = sums[c] + jnp.where(hit, rows[:, at : at + 1], 0.0)
    for c in range(3):
        ffd[c : c + 1, :] = jnp.sum(sums[c], axis=0, keepdims=True)

    sent_faces(STEPS - 1)

    @pl.when(w == 0)
    def _():
        owner_bytes(goes, owners - 1).wait_send()


def store_kernel(state, owned, state_out, owned_out, sem):
    copies = (
        pltpu.make_async_copy(state, state_out, sem.at[0]),
        pltpu.make_async_copy(owned, owned_out, sem.at[1]),
    )
    for copy in copies:
        copy.start()
    for copy in copies:
        copy.wait()


def solution(mesh):
    sizes = tuple(mesh.shape[name] for name in ("azim", "merid", "wall"))
    na, nm, nw = sizes
    group = nm * nw
    faces = (STEPS, 5, NV, FPTS, TILE)
    scratch = [
        pltpu.VMEM((NV, NSP, E), F32),
        pltpu.VMEM((NV, NSP, E), F32),
        pltpu.VMEM((NV * NV, NSP, E), BF16),
        pltpu.VMEM((3, NSP, E), BF16),
        pltpu.VMEM((NFP, E), BF16),
        pltpu.VMEM((3, NSP, NSP), F32),
        pltpu.VMEM((NSP, NFP), F32),
        pltpu.VMEM((4, TILE), I32),
        pltpu.VMEM((4, TILE), I32),
        pltpu.SMEM((PTS // FPTS,), I32),
        pltpu.VMEM((NV, 3, PTS), BF16),
        pltpu.VMEM((1, PTS), I32),
        pltpu.VMEM((1, na * group), I32),
        pltpu.VMEM((NFP, E), F32),
        pltpu.VMEM((NV, NFP, E), F32),
        pltpu.VMEM((NV, 3 * NSP, E), F32),
        pltpu.VMEM((NV, 3 * NSP, E), BF16),
        pltpu.VMEM((NV, NSP, E), F32),
        pltpu.VMEM((NV, NFP, E), F32),
        pltpu.VMEM((NV, 2 * NFP, E), BF16),
        pltpu.VMEM((NFP, 3 * NSP), BF16),
        pltpu.VMEM((3 * NSP, 3 * NSP), BF16),
        pltpu.VMEM((2 * NSP, 2 * NFP), BF16),
        pltpu.VMEM((2 * NFP, 2 * NFP), BF16),
        pltpu.VMEM((NV, NFP, E), F32),
        pltpu.VMEM((4, NV, FPTS, TILE), F32),
        pltpu.VMEM((5 * FPTS, TILE), F32),
        pltpu.VMEM((FPTS, NV * TILE), F32),
        pltpu.VMEM((TILE, TILE), F32),
        pltpu.VMEM((4, FPTS, TILE), I32),
        pltpu.VMEM(faces, F32),
        pltpu.VMEM(faces, F32),
        pltpu.VMEM((NV, FPTS, TILE), F32),
        pltpu.VMEM((3 * NSP, NV * TILE), BF16),
        pltpu.VMEM((8, PTS), F32),
        pltpu.VMEM((na * group, 2 * PTS), BF16),
        pltpu.VMEM((1, PTS), I32),
        pltpu.VMEM((1, PTS), F32),
        pltpu.VMEM((TILE, 2 * PTS), BF16),
        pltpu.VMEM((na * group, TILE), F32),
        pltpu.VMEM((na * nm, TILE), F32),
        pltpu.SemaphoreType.DMA((4,)),
        pltpu.SemaphoreType.DMA((3,)),
        pltpu.SemaphoreType.DMA((STEPS, 3)),
        pltpu.SemaphoreType.DMA((2,)),
        pltpu.SemaphoreType.REGULAR((3,)),
    ]
    hbm = pl.BlockSpec(memory_space=pltpu.HBM)
    vmem = pl.BlockSpec(memory_space=pltpu.VMEM)
    call = pl.pallas_call(
        functools.partial(kernel, sizes),
        out_shape=(pltpu.VMEM((NV, NSP, E), F32), pltpu.VMEM((3, BLOCK), F32)),
        in_specs=[hbm] * 13,
        out_specs=(vmem, vmem),
        scratch_shapes=scratch,
        compiler_params=pltpu.CompilerParams(
            collective_id=0, has_side_effects=True, vmem_limit_bytes=40 * 1024 * 1024
        ),
        name="adjoint_steps",
    )

    store = pl.pallas_call(
        store_kernel,
        out_shape=(
            jax.ShapeDtypeStruct((NV, NSP, E), F32),
            jax.ShapeDtypeStruct((3, BLOCK), F32),
        ),
        in_specs=[vmem] * 2,
        out_specs=(hbm, hbm),
        scratch_shapes=[pltpu.SemaphoreType.DMA((2,))],
        name="store_results",
    )

    def per_device(
        adjoint_in,
        source,
        jacobian,
        metric,
        penalty,
        deriv,
        interp,
        face_match,
        orientation,
        wall_faces,
        wall_geometry,
        lattice_cells,
        block_owner,
    ):
        operands = (
            adjoint_in.reshape(NV, NSP, E),
            source.reshape(NV, NSP, E),
            jacobian.reshape(NV * NV, NSP, E),
            metric.reshape(3, NSP, E),
            penalty.reshape(NFP, E),
            deriv,
            interp.T,
            face_match.reshape(4, TILE),
            orientation.reshape(4, TILE),
            wall_faces.reshape(-1),
            wall_geometry.reshape(3, NV, PTS).transpose(1, 0, 2),
            lattice_cells.reshape(1, PTS),
            block_owner.reshape(1, -1),
        )
        adjoint, owned = call(
            *(pltpu.with_memory_space_constraint(operand, pltpu.HBM) for operand in operands)
        )
        adjoint, owned = store(
            pltpu.with_memory_space_constraint(adjoint, pltpu.VMEM),
            pltpu.with_memory_space_constraint(owned, pltpu.VMEM),
        )
        return adjoint[None, None, None], owned

    placed = (
        P("azim", "merid", "wall", None, None, None),
        P("azim", "merid", "wall", None, None, None),
        P("azim", "merid", "wall", None, None, None, None),
        P("azim", "merid", "wall", None, None, None),
        P("azim", "merid", "wall", None, None),
        P(),
        P(),
        P("azim", "merid", "wall", None, None),
        P("azim", "merid", "wall", None, None),
        P("azim", "merid", None),
        P("azim", "merid", None, None, None),
        P("azim", "merid", None),
        P(),
    )
    return jax.shard_map(
        per_device,
        mesh=mesh,
        in_specs=placed,
        out_specs=(
            P("azim", "merid", "wall", None, None, None),
            P(None, ("azim", "merid", "wall")),
        ),
        check_vma=False,
    )
```
